512 devices in a mesh: shot: 64 (over y_hi, x, z), dom: 8 (over y_lo, core).
Axes of the slice: x: 4, y: 8 (y_hi: 2, y_lo: 4; y = y_hi * 4 + y_lo), z: 8, core: 2. Of those that a mesh axis runs over, the one named last changes fastest.
Arguments:
- kappa: float32 [128, 128, 128], P('dom'), may hold values from 0.08 to 0.18
- source_pair: bfloat16 [64, 2, 128, 128, 128], P('shot', None, 'dom'), may hold values from -6 to 6
- adjoint_pair: bfloat16 [64, 2, 128, 128, 128], P('shot', None, 'dom'), may hold values from -6 to 6
- wavelet: float32 [64, 4], P('shot'), may hold values from -6 to 6
- residuals: float32 [64, 4, 256], P('shot'), may hold values from -6 to 6
- source_cell: int32 [64, 3], P('shot'), may hold values from 0 to 127, as said below
- receiver_cells: int32 [64, 3, 256], P('shot'), may hold values from 0 to 127, as said below
Outputs:
- direction: float32 [128, 128, 128], P('dom', 'shot')
The draws below stay inside these ranges and needn't reach their ends.
Inputs may be any that keep to these rules, and one draw needn't show every extreme that they name: `source_cell`: each shot's source cell as depth, first lateral and second lateral index, below 128, 128 and 128 in turn; the first shot's source lies in the cell (0, 0, 0) and the last shot's in the cell (127, 127, 127). `receiver_cells`: each receiver's cell as depth, first lateral and second lateral index (dimension 1), below 128, 128 and 128 in turn; receivers may coincide; in every shot one receiver lies in the cell (0, 0, 0) and one in the cell (127, 127, 127).
All inputs are finite; a program needn't handle non-finite values.
Results may differ from the reference program's by a relative error of at most 0.0004.
Values sent between devices are 32-bit elements; how exact they have to be, the bound alone decides.
A program may use at most 192 MiB of HBM per device.

```python
import jax
import jax.numpy as jnp
from jax import lax

NX = 128
NY = 128
STEPS = 2
SEGS = 2
NREC = 256
SHOTS = 64
NZ = 128


def draw_source_cell(key, part):
    key = jax.random.fold_in(key, 11)
    keys = jax.random.split(key, 3)
    depth_pos = jax.random.randint(keys[0], (SHOTS, 1), 0, NZ)
    first_pos = jax.random.randint(keys[1], (SHOTS, 1), 0, NX)
    second_pos = jax.random.randint(keys[2], (SHOTS, 1), 0, NY)
    cells = jnp.concatenate((depth_pos, first_pos, second_pos), axis=1).astype(jnp.int32)
    corner = jnp.array([NZ - 1, NX - 1, NY - 1], jnp.int32)
    cells = cells.at[0].set(jnp.zeros((3,), jnp.int32))
    cells = cells.at[SHOTS - 1].set(corner)
    return cells


def draw_receiver_cells(key, part):
    key = jax.random.fold_in(key, 23)
    keys = jax.random.split(key, 3)
    depth_pos = jax.random.randint(keys[0], (SHOTS, 1, NREC), 0, NZ)
    first_pos = jax.random.randint(keys[1], (SHOTS, 1, NREC), 0, NX)
    second_pos = jax.random.randint(keys[2], (SHOTS, 1, NREC), 0, NY)
    cells = jnp.concatenate((depth_pos, first_pos, second_pos), axis=1).astype(jnp.int32)
    corner = jnp.array([NZ - 1, NX - 1, NY - 1], jnp.int32)
    cells = cells.at[:, :, 0].set(jnp.zeros((SHOTS, 3), jnp.int32))
    cells = cells.at[:, :, NREC - 1].set(jnp.broadcast_to(corner[None, :], (SHOTS, 3)))
    return cells


def block_scale(stream_key, shape, cuts, least, high):
    factor_of, own = 1.0, jax.random.fold_in(stream_key, 6)
    for axis_at, blocks in cuts:
        steps = jnp.exp(jax.random.uniform(jax.random.fold_in(own, axis_at), (blocks,), jnp.float32, least / len(cuts), high / len(cuts)))
        factor_of = factor_of * jnp.repeat(steps, shape[axis_at] // blocks).reshape([-1 if axis == axis_at else 1 for axis in range(len(shape))])
    return factor_of


def gaussian(key, shape, spread, bound, shards=(), dtype=jnp.bfloat16):
    entries = jax.random.normal(key, shape, jnp.float32) * spread
    if len(shards) > 0:
        entries = block_scale(key, shape, shards, -0.22, 0.18) * entries
    return jnp.clip(entries, min=-bound, max=bound).astype(dtype)


def setup_inputs(seed: int = 0) -> dict:
    key_of = jax.random.split(jax.random.key(seed), 8)
    return {
        "kappa": jnp.clip(0.08 + 0.10000001 * jax.random.uniform(key_of[0], (NZ, NX, NY), jnp.float32) ** block_scale(key_of[0], (NZ, NX, NY), ((0, 8),), -0.2, 0.2), 0.08, 0.18),
        "source_pair": gaussian(key_of[1], (SHOTS, 2, NZ, NX, NY), 1.0, 6.0, ((0, 64), (2, 8))),
        "adjoint_pair": gaussian(key_of[2], (SHOTS, 2, NZ, NX, NY), 1.0, 6.0, ((0, 64), (2, 8))),
        "wavelet": gaussian(key_of[3], (SHOTS, SEGS * STEPS), 1.0, 6.0, ((0, 64),), jnp.float32),
        "residuals": gaussian(key_of[4], (SHOTS, SEGS * STEPS, NREC), 1.0, 6.0, ((0, 64),), jnp.float32),
        "source_cell": draw_source_cell(jax.random.fold_in(key_of[7], 71), 0),
        "receiver_cells": draw_receiver_cells(jax.random.fold_in(key_of[7], 71), 0),
    }


COEFFS = (-205.0 / 72.0, 8.0 / 5.0, -1.0 / 5.0, 8.0 / 315.0, -1.0 / 560.0)
BINOMIAL = (0.0625, 0.25, 0.375, 0.25, 0.0625)

def laplace(field):
    depth, width, span = field.shape
    padded = jnp.pad(field, 4)
    summed = 3.0 * COEFFS[0] * field
    for shift in range(1, 5):
        summed = summed + COEFFS[shift] * (padded[4 + shift:4 + shift + depth, 4:4 + width, 4:4 + span] + padded[4 - shift:4 - shift + depth, 4:4 + width, 4:4 + span] + padded[4:4 + depth, 4 + shift:4 + shift + width, 4:4 + span] + padded[4:4 + depth, 4 - shift:4 - shift + width, 4:4 + span] + padded[4:4 + depth, 4:4 + width, 4 + shift:4 + shift + span] + padded[4:4 + depth, 4:4 + width, 4 - shift:4 - shift + span])
    return summed

def blur_axis(field, axis):
    count = field.shape[axis]
    widths = [(0, 0), (0, 0), (0, 0)]
    widths[axis] = (2, 2)
    padded = jnp.pad(field, widths)
    summed = jnp.zeros_like(field)
    for offset in range(5):
        summed = summed + BINOMIAL[offset] * lax.slice_in_dim(padded, offset, offset + count, axis=axis)
    return summed

def one_shot(kappa, source_two, adjoint_two, wave_row, residual_rows, cell, receivers):
    zeros = jnp.zeros(kappa.shape, jnp.float32)
    current_u = source_two[0].astype(jnp.float32)
    later_u = source_two[1].astype(jnp.float32)
    current_l = adjoint_two[0].astype(jnp.float32)
    later_l = adjoint_two[1].astype(jnp.float32)
    parts = []
    for segment in reversed(range(SEGS)):
        gradient = zeros
        for moment in reversed(range(segment * STEPS, (segment + 1) * STEPS)):
            curv_u = kappa * laplace(current_u)
            curv_l = kappa * laplace(current_l)
            source_term = zeros.at[cell[0], cell[1], cell[2]].add(wave_row[moment])
            receiver_term = zeros.at[receivers[0], receivers[1], receivers[2]].add(residual_rows[moment])
            earlier_u = 2.0 * current_u - later_u + curv_u + source_term
            earlier_l = 2.0 * current_l - later_l + curv_l + receiver_term
            gradient = gradient + current_l * (curv_u + source_term)
            later_u, current_u = (current_u, earlier_u)
            later_l, current_l = (current_l, earlier_l)
        parts.append(gradient)
    return parts[0] + parts[1]

def reference(kappa, source_pair, adjoint_pair, wavelet, residuals, source_cell, receiver_cells):

    def step_shot(carry, items):
        return (carry + one_shot(kappa, *items), None)
    summed, _ = lax.scan(step_shot, jnp.zeros(kappa.shape, jnp.float32), (source_pair, adjoint_pair, wavelet, residuals, source_cell, receiver_cells))
    smoothed = blur_axis(blur_axis(summed, 1), 2)
    power = jnp.mean(smoothed * smoothed)
    return -smoothed * lax.rsqrt(power + 1e-06)
```

```python
import functools

import jax
import jax.numpy as jnp
from jax import lax
from jax.experimental import pallas as pl
from jax.experimental.pallas import tpu as pltpu
from jax.sharding import PartitionSpec as P

MESH = pl.DeviceIdType.MESH
LEVELS = 4
HALO = 4
SCALE = 5040.0
RING = (8064.0, -1008.0, 128.0, -9.0)
CENTER = 3.0 * -14350.0
SHOT_PARTS = (2, 4, 8)
CHUNKS = 2
F32 = jnp.float32
BF16 = jnp.bfloat16


def split(value):
    high = value.astype(BF16)
    low = (value - high.astype(F32)).astype(BF16)
    return high, low


def band(size, weights):
    rows = lax.broadcasted_iota(jnp.int32, (size, size), 0)
    columns = lax.broadcasted_iota(jnp.int32, (size, size), 1)
    distance = jnp.abs(rows - columns)
    matrix = jnp.zeros((size, size), F32)
    for d, weight in enumerate(weights):
        matrix = jnp.where(distance == d, weight, matrix)
    return matrix


def dot(a, b):
    return jnp.dot(a, b, preferred_element_type=F32)


def wave_kernel(
    doms, kappa_hbm, source_hbm, adjoint_hbm, wave, residual, cell, receiver, out,
    kappa, given, field, total, spot, marks, row_side, column_side, blur_row, blur_column,
    load_sem, send_sem, recv_sem,
):
    depth, width, span = kappa.shape
    shot, dom = lax.axis_index("shot"), lax.axis_index("dom")
    core = dom % 2
    anchor = dom * depth

    loads = []
    for at, (source, target) in enumerate(
        (
            (source_hbm.at[0], given.at[0, 0]),
            (adjoint_hbm.at[0], given.at[1, 0]),
            (kappa_hbm, kappa),
            (source_hbm.at[1], given.at[0, 1]),
            (adjoint_hbm.at[1], given.at[1, 1]),
        )
    ):
        copy = pltpu.make_async_copy(source, target, load_sem.at[at])
        copy.start()
        loads.append(copy)

    barrier = pltpu.get_barrier_semaphore()

    @pl.when(dom > 0)
    def _():
        pl.semaphore_signal(barrier, inc=1, device_id=(shot, dom - 1), device_id_type=MESH)

    @pl.when(dom < doms - 1)
    def _():
        pl.semaphore_signal(barrier, inc=1, device_id=(shot, dom + 1), device_id_type=MESH)

    @pl.when(dom == 0)
    def _():
        field[:, :, 0:HALO] = jnp.zeros((2, LEVELS, HALO, width, span), F32)

    @pl.when(dom == doms - 1)
    def _():
        field[:, :, HALO + depth :] = jnp.zeros((2, LEVELS, HALO, width, span), F32)

    def beside(side):
        neighbour = dom + 2 * side - 1
        return neighbour, (neighbour >= 0) & (neighbour < doms)

    def halo_copy(which, level, side):
        neighbour, _ = beside(side)
        return pltpu.make_async_remote_copy(
            src_ref=field.at[which, level, pl.ds(HALO + (depth - HALO) * side, HALO)],
            dst_ref=field.at[which, level, pl.ds((HALO + depth) * (1 - side), HALO)],
            send_sem=send_sem.at[which, level, side],
            recv_sem=recv_sem.at[which, level, 1 - side],
            device_id=(shot, neighbour),
            device_id_type=MESH,
        )

    def halo_send(which, level, side):
        @pl.when(beside(side)[1])
        def _():
            halo_copy(which, level, side).start()

    def halo_wait(which, level, side):
        @pl.when(beside(side)[1])
        def _():
            pltpu.make_async_remote_copy(
                src_ref=field.at[which, level, pl.ds(HALO + (depth - HALO) * side, HALO)],
                dst_ref=field.at[which, level, pl.ds((HALO + depth) * side, HALO)],
                send_sem=send_sem.at[which, level, side],
                recv_sem=recv_sem.at[which, level, side],
                device_id=(shot, beside(side)[0]),
                device_id_type=MESH,
            ).wait_recv()

    neighbours = jnp.where(dom > 0, 1, 0) + jnp.where(dom < doms - 1, 1, 0)
    for which in (0, 1):
        loads[which].wait()
        for side in (0, 1):
            start = (depth - HALO) * side
            field[which, LEVELS - 1, start + HALO : start + 2 * HALO] = given[
                which, 0, start : start + HALO
            ].astype(F32)
        if which == 0:
            pl.semaphore_wait(barrier, neighbours)
        for turn in (0, 1):
            halo_send(which, LEVELS - 1, turn ^ core)
    for which in (0, 1):

        @pl.loop(HALO, depth - HALO)
        def _(z):
            field[which, LEVELS - 1, z + HALO] = given[which, 0, z].astype(F32)

    taps = band(width, (0.0,) + RING).astype(BF16)
    row_side[...] = jnp.concatenate((taps, taps), axis=1)
    taps = band(span, (0.0,) + RING).astype(BF16)
    lines = lax.broadcasted_iota(jnp.int32, (span, receiver.shape[1]), 0)
    for level in range(1, LEVELS):
        spread = jnp.where(lines == receiver[2:3, :], residual[level : level + 1, :], 0.0)
        high, low = split(jnp.transpose(spread))
        column_side[level] = jnp.concatenate((taps, taps, high, low), axis=0)
    first = lax.broadcasted_iota(jnp.int32, (width, span), 0) == cell[1]
    second = lax.broadcasted_iota(jnp.int32, (width, span), 1) == cell[2]
    spot[...] = jnp.where(first & second, 1.0, 0.0)
    lines = lax.broadcasted_iota(jnp.int32, (width, receiver.shape[1]), 0)

    @pl.loop(0, depth)
    def _(z):
        hit = (lines == receiver[1:2, :]) & (receiver[0:1, :] == anchor + z)
        marks[z] = jnp.where(hit, 1.0, 0.0).astype(BF16)

    parts_y, parts_x, parts_z = SHOT_PARTS
    rows = width // (parts_y * parts_x * parts_z)
    place = lax.broadcasted_iota(jnp.int32, (width, width), 0)
    row = place % rows
    y_hi = place // rows % parts_y
    z_at = place // (rows * parts_y) % parts_z
    x_at = place // (rows * parts_y * parts_z)
    wanted = ((y_hi * parts_x + x_at) * parts_z + z_at) * rows + row
    distance = jnp.abs(wanted - lax.broadcasted_iota(jnp.int32, (width, width), 1))
    taps = jnp.zeros((width, width), F32)
    for d, weight in enumerate((6.0, 4.0, 1.0)):
        taps = jnp.where(distance == d, weight / 16.0, taps)
    taps = taps.astype(BF16)
    blur_row[...] = jnp.concatenate((taps, taps), axis=1)
    taps = band(span, (0.375, 0.25, 0.0625)).astype(BF16)
    blur_column[...] = jnp.concatenate((taps, taps), axis=0)

    def advance(which, level, z):
        current = field[which, level, z + HALO]
        if level == LEVELS - 1:
            high = given[which, 0, z]
            upright, flat, skip = high, [high], span
            left = row_side[:, :width]
        else:
            high, low = split(current)
            upright, flat, skip = jnp.concatenate((high, low), axis=0), [high, low], 0
            left = row_side[...]
        if which == 1:
            flat = flat + [marks[z], marks[z]]
            right = column_side[level, skip:]
        else:
            right = column_side[1, skip : 2 * span]
        if len(flat) > 1:
            flat = jnp.concatenate(flat, axis=1)
        else:
            flat = flat[0]
        if which == 1:
            cut = 2 * span - skip
            lateral = dot(left, upright) + dot(flat[:, :cut], right[:cut])
            inject = dot(flat[:, cut:], right[cut:])
        else:
            lateral = dot(left, upright) + dot(flat, right)
            inject = jnp.where(cell[0] == anchor + z, wave[level], 0.0) * spot[...]
        summed = lateral + CENTER * current
        for shift in range(1, HALO + 1):
            summed = summed + RING[shift - 1] * (
                field[which, level, z + HALO + shift] + field[which, level, z + HALO - shift]
            )
        term = kappa[z] * (summed * (1.0 / SCALE)) + inject
        if which == 0:
            part = field[1, level, z + HALO] * term
            if level < LEVELS - 1:
                part = part + total[z]
            if level > 0:
                total[z] = part
            else:
                high, low = split(part)
                part = dot(jnp.concatenate((high, low), axis=1), blur_column[...])
                high, low = split(part)
                out[z] = dot(blur_row[...], jnp.concatenate((high, low), axis=0))
        if level > 0:
            if level == LEVELS - 1:
                later = given[which, 1, z].astype(F32)
            else:
                later = field[which, level + 1, z + HALO]
            field[which, level - 1, z + HALO] = 2.0 * current - later + term

    def run(which, level, start, count):
        @pl.loop(0, count)
        def _(i):
            advance(which, level, start + i)

    for load in loads[2:]:
        load.wait()
    for level in reversed(range(LEVELS)):
        fields = (0, 1) if level > 0 else (0,)
        if level == LEVELS - 1:
            for which in fields:
                run(which, level, HALO, depth - 2 * HALO)
        for turn in (0, 1):
            side = turn ^ core
            for which in fields:
                halo_wait(which, level, side)
                run(which, level, (depth - HALO) * side, HALO)
                if level > 1 or (level == 1 and which == 0):
                    halo_send(which, level - 1, side)
        if level < LEVELS - 1:
            for which in fields:
                run(which, level, HALO, depth - 2 * HALO)

    for level in reversed(range(LEVELS)):
        for which in (0, 1) if level > 0 else (0,):
            for side in (0, 1):

                @pl.when(beside(side)[1])
                def _():
                    halo_copy(which, level, side).wait_send()


def sum_kernel(
    doms, cells, part, out,
    x_in, z_out, z_in, y_out, y_in, power_out, power_in,
    x_send, x_recv, z_send, z_recv, y_send, y_recv, p_send, p_recv,
):
    depth, width, span = part.shape
    shot, dom = lax.axis_index("shot"), lax.axis_index("dom")
    parts_y, parts_x, parts_z = SHOT_PARTS
    rows = width // (parts_y * parts_x * parts_z)
    z_at, x_at, y_at = shot % parts_z, shot // parts_z % parts_x, shot // (parts_z * parts_x)
    layers = depth // CHUNKS
    stripe = width // parts_x

    def by_x(step):
        return ((y_at * parts_x + (x_at + step) % parts_x) * parts_z + z_at, dom)

    def by_z(step):
        return ((y_at * parts_x + x_at) * parts_z + (z_at + step) % parts_z, dom)

    def by_xy(step):
        at = (y_at * parts_x + x_at + step) % (parts_x * parts_y)
        return (at * parts_z + z_at, dom)

    def by_dom(step):
        return (shot, (dom + step) % doms)

    barrier = pltpu.get_barrier_semaphore()
    peers = [by_dom(step) for step in range(1, doms)]
    peers += [by_z(step) for step in range(1, parts_z)]
    peers += [by_xy(step) for step in range(1, parts_x * parts_y)]
    for peer in peers:
        pl.semaphore_signal(barrier, inc=1, device_id=peer, device_id_type=MESH)
    pl.semaphore_wait(barrier, len(peers))

    def send(source, target, send_sem, recv_sem, peer):
        copy = pltpu.make_async_remote_copy(
            src_ref=source,
            dst_ref=target,
            send_sem=send_sem,
            recv_sem=recv_sem,
            device_id=peer,
            device_id_type=MESH,
        )
        copy.start()
        return copy

    sent = []
    x_copies = [[] for _ in range(CHUNKS)]
    for chunk in range(CHUNKS):
        for step in range(1, parts_x):
            start = pl.multiple_of((x_at + step) % parts_x * stripe, stripe)
            x_copies[chunk].append(
                send(
                    part.at[pl.ds(chunk * layers, layers), pl.ds(start, stripe)],
                    x_in.at[chunk, step - 1],
                    x_send.at[chunk, step - 1],
                    x_recv.at[chunk, step - 1],
                    by_x(step),
                )
            )
    count = layers * stripe
    to = lax.broadcasted_iota(jnp.int32, (count, count), 0)
    row = to % rows
    layer = to // rows % layers
    y_hi = to // (rows * layers) % parts_y
    z_of = to // (rows * layers * parts_y)
    wanted = ((layer * parts_z + z_of) * parts_y + y_hi) * rows + row
    order = wanted == lax.broadcasted_iota(jnp.int32, (count, count), 1)
    order = jnp.where(order, 1.0, 0.0).astype(BF16)
    own = pl.multiple_of(x_at * stripe, stripe)
    z_copies = [[] for _ in range(CHUNKS)]
    for chunk in range(CHUNKS):
        summed = part[pl.ds(chunk * layers, layers), pl.ds(own, stripe)]
        for step in range(1, parts_x):
            x_copies[chunk][step - 1].wait_recv()
            summed = summed + x_in[chunk, step - 1]
        high, low = split(summed.reshape(count, span))
        moved = dot(order, high) + dot(order, low)
        z_out[chunk] = moved.reshape(parts_z, count // parts_z, span)
        for step in range(1, parts_z):
            z_copies[chunk].append(
                send(
                    z_out.at[chunk, (z_at + step) % parts_z],
                    z_in.at[chunk, step - 1],
                    z_send.at[chunk, step - 1],
                    z_recv.at[chunk, step - 1],
                    by_z(step),
                )
            )
    block = rows * layers
    for chunk in range(CHUNKS):
        summed = z_out[chunk, z_at]
        for step in range(1, parts_z):
            z_copies[chunk][step - 1].wait_recv()
            summed = summed + z_in[chunk, step - 1]
        for y_hi in range(parts_y):
            y_out[y_hi, chunk * block : (chunk + 1) * block] = summed[
                y_hi * block : (y_hi + 1) * block
            ]
    summed = y_out[y_at]
    y_copies = []
    for step in range(1, parts_y):
        y_copies.append(
            send(
                y_out.at[(y_at + step) % parts_y],
                y_in.at[step - 1],
                y_send.at[step - 1],
                y_recv.at[step - 1],
                by_xy(step * parts_x),
            )
        )
    for step in range(1, parts_y):
        y_copies[step - 1].wait_recv()
        summed = summed + y_in[step - 1]
    squares = summed * summed
    power = squares[0:8]
    for at in range(8, rows * depth, 8):
        power = power + squares[at : at + 8]
    p_copies = []
    for stage, (size, by) in enumerate(
        ((doms, by_dom), (parts_z, by_z), (parts_x * parts_y, by_xy))
    ):
        power_out[stage] = power
        now = [
            send(
                power_out.at[stage],
                power_in.at[stage, step - 1],
                p_send.at[stage, step - 1],
                p_recv.at[stage, step - 1],
                by(step),
            )
            for step in range(1, size)
        ]
        for step in range(1, size):
            now[step - 1].wait_recv()
            power = power + power_in[stage, step - 1]
        p_copies += now
    power = jnp.sum(power)
    out[...] = -summed * lax.rsqrt(jnp.full((1, 1), power) * (1.0 / cells) + 1e-6)
    for copies in x_copies + z_copies + [y_copies, p_copies]:
        for copy in copies:
            copy.wait_send()


def per_device(doms, kappa, source_pair, adjoint_pair, wavelet, residuals, source_cell, receiver_cells):
    depth, width, span = kappa.shape
    receivers = receiver_cells.shape[2]
    parts_y, parts_x, parts_z = SHOT_PARTS
    layers = depth // CHUNKS
    rows = width // (parts_y * parts_x * parts_z)
    plane = (width, span)
    hbm = pl.BlockSpec(memory_space=pl.ANY)
    vmem = pl.BlockSpec(memory_space=pltpu.VMEM)
    smem = pl.BlockSpec(memory_space=pltpu.SMEM)
    dma = pltpu.SemaphoreType.DMA
    part = pl.pallas_call(
        functools.partial(wave_kernel, doms),
        out_shape=jax.ShapeDtypeStruct(kappa.shape, F32),
        in_specs=[hbm, hbm, hbm, smem, vmem, smem, vmem],
        out_specs=vmem,
        scratch_shapes=[
            pltpu.VMEM(kappa.shape, F32),
            pltpu.VMEM((2, 2, depth) + plane, BF16),
            pltpu.VMEM((2, LEVELS, depth + 2 * HALO) + plane, F32),
            pltpu.VMEM(kappa.shape, F32),
            pltpu.VMEM(plane, F32),
            pltpu.VMEM((depth, width, receivers), BF16),
            pltpu.VMEM((width, 2 * width), BF16),
            pltpu.VMEM((LEVELS, 2 * span + 2 * receivers, span), BF16),
            pltpu.VMEM((width, 2 * width), BF16),
            pltpu.VMEM((2 * span, span), BF16),
            dma((5,)),
            dma((2, LEVELS, 2)),
            dma((2, LEVELS, 2)),
        ],
        compiler_params=pltpu.CompilerParams(
            collective_id=0, has_side_effects=True, vmem_limit_bytes=40 * 2**20
        ),
    )(
        kappa,
        source_pair[0],
        adjoint_pair[0],
        wavelet[0],
        residuals[0],
        source_cell[0],
        receiver_cells[0],
    )
    stages = 3
    most = max(doms, parts_z, parts_x * parts_y) - 1
    stripe = width // parts_x
    piece = layers * stripe // parts_z
    direction = pl.pallas_call(
        functools.partial(sum_kernel, doms, float(depth * doms * width * span)),
        out_shape=jax.ShapeDtypeStruct((depth * rows, span), F32),
        in_specs=[vmem],
        out_specs=vmem,
        scratch_shapes=[
            pltpu.VMEM((CHUNKS, parts_x - 1, layers, stripe, span), F32),
            pltpu.VMEM((CHUNKS, parts_z, piece, span), F32),
            pltpu.VMEM((CHUNKS, parts_z - 1, piece, span), F32),
            pltpu.VMEM((parts_y, depth * rows, span), F32),
            pltpu.VMEM((parts_y - 1, depth * rows, span), F32),
            pltpu.VMEM((stages, 8, span), F32),
            pltpu.VMEM((stages, most, 8, span), F32),
            dma((CHUNKS, parts_x - 1)),
            dma((CHUNKS, parts_x - 1)),
            dma((CHUNKS, parts_z - 1)),
            dma((CHUNKS, parts_z - 1)),
            dma((parts_y - 1,)),
            dma((parts_y - 1,)),
            dma((stages, most)),
            dma((stages, most)),
        ],
        compiler_params=pltpu.CompilerParams(
            collective_id=1, has_side_effects=True, vmem_limit_bytes=40 * 2**20
        ),
    )(part)
    return direction.reshape(depth, rows, span)


def solution(mesh):
    return jax.shard_map(
        functools.partial(per_device, mesh.shape["dom"]),
        mesh=mesh,
        in_specs=(
            P("dom", None, None),
            P("shot", None, "dom", None, None),
            P("shot", None, "dom", None, None),
            P("shot", None),
            P("shot", None, None),
            P("shot", None),
            P("shot", None, None),
        ),
        out_specs=P("dom", "shot", None),
        check_vma=False,
    )
```

```python
import functools

import jax
import jax.numpy as jnp
from jax import lax
from jax.experimental import pallas as pl
from jax.experimental.pallas import tpu as pltpu
from jax.sharding import PartitionSpec as P

MESH = pl.DeviceIdType.MESH
LEVELS = 4
HALO = 4
SCALE = 5040.0
RING = (8064.0, -1008.0, 128.0, -9.0)
CENTER = 3.0 * -14350.0
SHOT_PARTS = (2, 4, 8)
F32 = jnp.float32
BF16 = jnp.bfloat16


def split(value):
    high = value.astype(BF16)
    low = (value - high.astype(F32)).astype(BF16)
    return high, low


def band(size, weights):
    rows = lax.broadcasted_iota(jnp.int32, (size, size), 0)
    columns = lax.broadcasted_iota(jnp.int32, (size, size), 1)
    distance = jnp.abs(rows - columns)
    matrix = jnp.zeros((size, size), F32)
    for d, weight in enumerate(weights):
        matrix = jnp.where(distance == d, weight, matrix)
    return matrix


def twice(matrix, axis):
    matrix = matrix.astype(BF16)
    return jnp.concatenate((matrix, matrix), axis=axis)


def dot(a, b):
    return jnp.dot(a, b, preferred_element_type=F32)


def rows_of(blocks):
    return jnp.concatenate(blocks, axis=0)


def columns_of(blocks):
    return jnp.concatenate(blocks, axis=1)


def kernel(
    doms, cells,
    kappa_hbm, source_hbm, adjoint_hbm, wave, residual, cell, receiver, out,
    kappa, given, fields, totals, part, spot, marks, row_side, column_side, inject_side,
    blur_row, blur_column, order,
    x_in, z_out, z_in, y_out, y_in, power_out, power_in,
    load_sem, halo_send, halo_recv,
    x_send, x_recv, z_send, z_recv, y_send, y_recv, p_send, p_recv,
):
    depth, width, span = kappa.shape
    chunks = depth // HALO
    shot, dom = lax.axis_index("shot"), lax.axis_index("dom")
    core = dom % 2
    anchor = dom * depth
    parts_y, parts_x, parts_z = SHOT_PARTS
    rows = width // (parts_y * parts_x * parts_z)
    z_at, x_at, y_at = shot % parts_z, shot // parts_z % parts_x, shot // (parts_z * parts_x)
    stripe = width // parts_x

    def by_x(step):
        return ((y_at * parts_x + (x_at + step) % parts_x) * parts_z + z_at, dom)

    def by_z(step):
        return ((y_at * parts_x + x_at) * parts_z + (z_at + step) % parts_z, dom)

    def by_y(step):
        at = (y_at * doms + dom + step) % (parts_y * doms)
        return ((at // doms * parts_x + x_at) * parts_z + z_at, at % doms)

    loads = []
    for at, (source, target) in enumerate(
        (
            (source_hbm.at[0], given[0][0]),
            (adjoint_hbm.at[0], given[1][0]),
            (kappa_hbm, kappa),
            (source_hbm.at[1], given[0][1]),
            (adjoint_hbm.at[1], given[1][1]),
        )
    ):
        copy = pltpu.make_async_copy(source, target, load_sem.at[at])
        copy.start()
        loads.append(copy)

    barrier = pltpu.get_barrier_semaphore()
    stages = (
        [by_y(step) for step in range(1, parts_y * doms)],
        [by_z(step) for step in range(1, parts_z)],
        [by_x(step) for step in range(1, parts_x)],
    )
    peers = [peer for stage in stages for peer in stage]
    for peer in peers:
        pl.semaphore_signal(barrier, inc=1, device_id=peer, device_id_type=MESH)

    @pl.when(dom == 0)
    def _():
        for which in (0, 1):
            for level in range(LEVELS):
                fields[which][level][0:HALO] = jnp.zeros((HALO, width, span), F32)

    @pl.when(dom == doms - 1)
    def _():
        for which in (0, 1):
            for level in range(LEVELS):
                fields[which][level][HALO + depth :] = jnp.zeros((HALO, width, span), F32)

    def beside(side):
        neighbour = dom + 2 * side - 1
        return neighbour, (neighbour >= 0) & (neighbour < doms)

    def halo_copy(which, level, side, landing):
        field = fields[which][level]
        return pltpu.make_async_remote_copy(
            src_ref=field.at[pl.ds(HALO + (depth - HALO) * side, HALO)],
            dst_ref=field.at[pl.ds((HALO + depth) * landing, HALO)],
            send_sem=halo_send.at[which, level, side],
            recv_sem=halo_recv.at[which, level, landing],
            device_id=(shot, beside(side)[0]),
            device_id_type=MESH,
        )

    def halo_start(which, level, side):
        @pl.when(beside(side)[1])
        def _():
            halo_copy(which, level, side, 1 - side).start()

    def halo_wait(which, level, side):
        @pl.when(beside(side)[1])
        def _():
            halo_copy(which, level, side, side).wait_recv()

    for which in (0, 1):
        loads[which].wait()
        field = fields[which][LEVELS - 1]
        for start in (0, depth - HALO):
            field[start + HALO : start + 2 * HALO] = given[which][0][
                start : start + HALO
            ].astype(F32)
        if which == 0:
            pl.semaphore_wait(barrier, len(peers))
        for turn in (0, 1):
            halo_start(which, LEVELS - 1, turn ^ core)
    for which in (0, 1):
        fields[which][LEVELS - 1][2 * HALO : depth] = given[which][0][
            HALO : depth - HALO
        ].astype(F32)

    row_side[...] = twice(band(width, (0.0,) + RING), 1)
    column_side[...] = twice(band(span, (0.0,) + RING), 0)
    first = lax.broadcasted_iota(jnp.int32, (width, span), 0) == cell[1]
    second = lax.broadcasted_iota(jnp.int32, (width, span), 1) == cell[2]
    spot[...] = jnp.where(first & second, 1.0, 0.0)
    lines = lax.broadcasted_iota(jnp.int32, (span, receiver.shape[2]), 0)
    for level in range(1, LEVELS):
        spread = jnp.where(lines == receiver[2], residual[level : level + 1, :], 0.0)
        inject_side[level] = columns_of(split(jnp.transpose(spread)))
    lines = lax.broadcasted_iota(jnp.int32, (width, receiver.shape[2]), 0)

    @pl.loop(0, depth)
    def _(z):
        hit = (lines == receiver[1]) & (receiver[0] == anchor + z)
        marks[z] = jnp.where(hit, 1.0, 0.0).astype(BF16)

    place = lax.broadcasted_iota(jnp.int32, (width, width), 0)
    row = place % rows
    y_hi = place // rows % parts_y
    z_of = place // (rows * parts_y) % parts_z
    x_of = place // (rows * parts_y * parts_z)
    wanted = ((y_hi * parts_x + x_of) * parts_z + z_of) * rows + row
    distance = jnp.abs(wanted - lax.broadcasted_iota(jnp.int32, (width, width), 1))
    taps = jnp.zeros((width, width), F32)
    for d, weight in enumerate((0.375, 0.25, 0.0625)):
        taps = jnp.where(distance == d, weight, taps)
    blur_row[...] = twice(taps, 1)
    blur_column[...] = twice(band(span, (0.375, 0.25, 0.0625)), 0)
    count = HALO * stripe
    place = lax.broadcasted_iota(jnp.int32, (count, count), 0)
    row = place % rows
    layer = place // rows % HALO
    y_hi = place // (rows * HALO) % parts_y
    z_of = place // (rows * HALO * parts_y)
    wanted = ((layer * parts_z + z_of) * parts_y + y_hi) * rows + row
    hit = wanted == lax.broadcasted_iota(jnp.int32, (count, count), 1)
    order[...] = twice(jnp.where(hit, 1.0, 0.0), 1)

    def both_sides(blocks, left, right):
        flat = rows_of([columns_of(block) for block in blocks])
        upright = columns_of([rows_of(block) for block in blocks])
        flat, upright = dot(flat, right), dot(left, upright)
        return [
            flat[at * width : (at + 1) * width] + upright[:, at * span : (at + 1) * span]
            for at in range(len(blocks))
        ]

    def advance(which, level, start):
        field = fields[which][level]
        layers = range(HALO)
        if level == LEVELS - 1:
            blocks = [(given[which][0][start + at],) for at in layers]
            lateral = both_sides(blocks, row_side[:, :width], column_side[:span])
        else:
            blocks = [split(field[start + at + HALO]) for at in layers]
            lateral = both_sides(blocks, row_side[...], column_side[...])
        if which == 1:
            inject = dot(rows_of([marks[start + at] for at in layers]), inject_side[level])
            inject = inject[:, :span] + inject[:, span:]
            inject = [inject[at * width : (at + 1) * width] for at in layers]
        else:
            inject = [
                jnp.where(cell[0] == anchor + start + at, wave[level], 0.0) * spot[...]
                for at in layers
            ]
        blurred = []
        for at in layers:
            z = start + at
            current = field[z + HALO]
            summed = lateral[at] + CENTER * current
            for shift in range(1, HALO + 1):
                summed = summed + RING[shift - 1] * (
                    field[z + HALO + shift] + field[z + HALO - shift]
                )
            term = kappa[z] * (summed * (1.0 / SCALE)) + inject[at]
            if which == 0:
                product = fields[1][level][z + HALO] * term
                if level < LEVELS - 1:
                    product = product + totals[level][z]
                if level > 0:
                    totals[level - 1][z] = product
                else:
                    blurred.append(product)
            if level > 0:
                if level == LEVELS - 1:
                    later = given[which][1][z].astype(F32)
                else:
                    later = fields[which][level + 1][z + HALO]
                fields[which][level - 1][z + HALO] = 2.0 * current - later + term
        return blurred

    def blur(blurred, start):
        flat = dot(rows_of([columns_of(split(at)) for at in blurred]), blur_column[...])
        blocks = [flat[at * width : (at + 1) * width] for at in range(HALO)]
        upright = dot(blur_row[...], columns_of([rows_of(split(at)) for at in blocks]))
        for at in range(HALO):
            part[start + at] = upright[:, at * span : (at + 1) * span]

    def send(source, target, send_sem, recv_sem, peer):
        copy = pltpu.make_async_remote_copy(
            src_ref=source,
            dst_ref=target,
            send_sem=send_sem,
            recv_sem=recv_sem,
            device_id=peer,
            device_id_type=MESH,
        )
        copy.start()
        return copy

    for load in loads[2:]:
        load.wait()
    for level in reversed(range(1, LEVELS)):
        if level == LEVELS - 1:
            for which in (0, 1):

                @pl.loop(HALO, depth - HALO, step=HALO)
                def _(start):
                    advance(which, level, start)

        @pl.loop(0, 2)
        def _(turn):
            side = turn ^ core
            for which in (0, 1):
                halo_wait(which, level, side)
                advance(which, level, (depth - HALO) * side)
                if level > 1 or which == 0:
                    halo_start(which, level - 1, side)

        if level < LEVELS - 1:
            for which in (0, 1):

                @pl.loop(HALO, depth - HALO, step=HALO)
                def _(start):
                    advance(which, level, start)

    starts = [HALO * at for at in range(1, chunks - 1)]
    starts += [(depth - HALO) * (1 - core), (depth - HALO) * core]
    x_copies, z_copies, y_copies, p_copies = ([[] for _ in starts] for _ in range(4))
    for chunk, start in enumerate(starts):
        if chunk >= chunks - 2:
            halo_wait(0, 0, (1 - core) if chunk == chunks - 2 else core)
        blur(advance(0, 0, start), start)
        for step in range(1, parts_x):
            place = pl.multiple_of((x_at + step) % parts_x * stripe, stripe)
            x_copies[chunk].append(
                send(
                    part.at[pl.ds(start, HALO), pl.ds(place, stripe)],
                    x_in.at[chunk, step - 1],
                    x_send.at[chunk, step - 1],
                    x_recv.at[chunk, step - 1],
                    by_x(step),
                )
            )
    own = pl.multiple_of(x_at * stripe, stripe)
    for chunk, start in enumerate(starts):
        summed = part[pl.ds(start, HALO), pl.ds(own, stripe)]
        for step in range(1, parts_x):
            x_copies[chunk][step - 1].wait_recv()
            summed = summed + x_in[chunk, step - 1]
        moved = dot(order[...], rows_of(split(summed.reshape(count, span))))
        z_out[chunk] = moved.reshape(parts_z, count // parts_z, span)
        for step in range(1, parts_z):
            z_copies[chunk].append(
                send(
                    z_out.at[chunk, (z_at + step) % parts_z],
                    z_in.at[chunk, step - 1],
                    z_send.at[chunk, step - 1],
                    z_recv.at[chunk, step - 1],
                    by_z(step),
                )
            )
    block = rows * HALO
    for chunk in range(chunks):
        summed = z_out[chunk, z_at]
        for step in range(1, parts_z):
            z_copies[chunk][step - 1].wait_recv()
            summed = summed + z_in[chunk, step - 1]
        y_out[chunk] = summed.reshape(parts_y, block, span)
        for step in range(1, parts_y):
            y_copies[chunk].append(
                send(
                    y_out.at[chunk, (y_at + step) % parts_y],
                    y_in.at[chunk, step - 1],
                    y_send.at[chunk, step - 1],
                    y_recv.at[chunk, step - 1],
                    by_y(step * doms),
                )
            )
    pieces = []
    power = jnp.zeros((block, span), F32)
    for chunk in range(chunks):
        summed = y_out[chunk, y_at]
        for step in range(1, parts_y):
            y_copies[chunk][step - 1].wait_recv()
            summed = summed + y_in[chunk, step - 1]
        pieces.append(summed)
        power = power + summed * summed
    for stage, peers in enumerate(stages):
        power_out[stage] = power
        now = [
            send(
                power_out.at[stage],
                power_in.at[stage, step],
                p_send.at[stage, step],
                p_recv.at[stage, step],
                peer,
            )
            for step, peer in enumerate(peers)
        ]
        for step, copy in enumerate(now):
            copy.wait_recv()
            power = power + power_in[stage, step]
        p_copies[0] += now
    scale = lax.rsqrt(jnp.full((1, 1), jnp.sum(power)) * (1.0 / cells) + 1e-6)
    for start, piece in zip(starts, pieces, strict=True):
        place = start * rows
        if not isinstance(place, int):
            place = pl.multiple_of(place, block)
        out[pl.ds(place, block)] = -piece * scale

    for copies in x_copies + z_copies + y_copies + p_copies:
        for copy in copies:
            copy.wait_send()
    for level in reversed(range(LEVELS)):
        for which in (0, 1) if level > 0 else (0,):
            for side in (0, 1):

                @pl.when(beside(side)[1])
                def _():
                    halo_copy(which, level, side, 1 - side).wait_send()


def per_device(doms, kappa, source_pair, adjoint_pair, wavelet, residuals, source_cell, receiver_cells):
    depth, width, span = kappa.shape
    receivers = receiver_cells.shape[2]
    parts_y, parts_x, parts_z = SHOT_PARTS
    rows = width // (parts_y * parts_x * parts_z)
    chunks = depth // HALO
    stripe = width // parts_x
    piece = HALO * stripe // parts_z
    block = rows * HALO
    most = max(doms * parts_y, parts_z, parts_x) - 1
    hbm = pl.BlockSpec(memory_space=pl.ANY)
    vmem = pl.BlockSpec(memory_space=pltpu.VMEM)
    smem = pl.BlockSpec(memory_space=pltpu.SMEM)
    dma = pltpu.SemaphoreType.DMA
    slab = pltpu.VMEM(kappa.shape, F32)
    padded = pltpu.VMEM((depth + 2 * HALO, width, span), F32)
    first = pltpu.VMEM(kappa.shape, BF16)
    direction = pl.pallas_call(
        functools.partial(kernel, doms, float(depth * doms * width * span)),
        out_shape=jax.ShapeDtypeStruct((depth * rows, span), F32),
        in_specs=[hbm, hbm, hbm, smem, vmem, smem, vmem],
        out_specs=vmem,
        scratch_shapes=[
            slab,
            [[first] * 2] * 2,
            [[padded] * LEVELS] * 2,
            [slab] * (LEVELS - 1),
            slab,
            pltpu.VMEM((width, span), F32),
            pltpu.VMEM((depth, width, receivers), BF16),
            pltpu.VMEM((width, 2 * width), BF16),
            pltpu.VMEM((2 * span, span), BF16),
            pltpu.VMEM((LEVELS, receivers, 2 * span), BF16),
            pltpu.VMEM((width, 2 * width), BF16),
            pltpu.VMEM((2 * span, span), BF16),
            pltpu.VMEM((HALO * stripe, 2 * HALO * stripe), BF16),
            pltpu.VMEM((chunks, parts_x - 1, HALO, stripe, span), F32),
            pltpu.VMEM((chunks, parts_z, piece, span), F32),
            pltpu.VMEM((chunks, parts_z - 1, piece, span), F32),
            pltpu.VMEM((chunks, parts_y, block, span), F32),
            pltpu.VMEM((chunks, parts_y - 1, block, span), F32),
            pltpu.VMEM((3, block, span), F32),
            pltpu.VMEM((3, most, block, span), F32),
            dma((5,)),
            dma((2, LEVELS, 2)),
            dma((2, LEVELS, 2)),
            dma((chunks, parts_x - 1)),
            dma((chunks, parts_x - 1)),
            dma((chunks, parts_z - 1)),
            dma((chunks, parts_z - 1)),
            dma((chunks, parts_y - 1)),
            dma((chunks, parts_y - 1)),
            dma((3, most)),
            dma((3, most)),
        ],
        compiler_params=pltpu.CompilerParams(
            collective_id=0, has_side_effects=True, vmem_limit_bytes=60 * 2**20
        ),
    )(
        kappa,
        source_pair[0],
        adjoint_pair[0],
        wavelet[0],
        residuals[0],
        source_cell[0],
        jnp.transpose(receiver_cells, (1, 0, 2)),
    )
    return direction.reshape(depth, rows, span)


def solution(mesh):
    return jax.shard_map(
        functools.partial(per_device, mesh.shape["dom"]),
        mesh=mesh,
        in_specs=(
            P("dom", None, None),
            P("shot", None, "dom", None, None),
            P("shot", None, "dom", None, None),
            P("shot", None),
            P("shot", None, None),
            P("shot", None),
            P("shot", None, None),
        ),
        out_specs=P("dom", "shot", None),
        check_vma=False,
    )
```

```python
import functools

import jax
import jax.numpy as jnp
from jax import lax
from jax.experimental import pallas as pl
from jax.experimental.pallas import tpu as pltpu
from jax.sharding import PartitionSpec as P

MESH = pl.DeviceIdType.MESH
LEVELS = 4
HALO = 4
SCALE = 5040.0
RING = (8064.0, -1008.0, 128.0, -9.0)
CENTER = 3.0 * -14350.0
SHOT_PARTS = (2, 4, 8)
F32 = jnp.float32
BF16 = jnp.bfloat16


def split(value):
    high = value.astype(BF16)
    low = (value - high.astype(F32)).astype(BF16)
    return high, low


def band(size, weights):
    rows = lax.broadcasted_iota(jnp.int32, (size, size), 0)
    columns = lax.broadcasted_iota(jnp.int32, (size, size), 1)
    distance = jnp.abs(rows - columns)
    matrix = jnp.zeros((size, size), F32)
    for d, weight in enumerate(weights):
        matrix = jnp.where(distance == d, weight, matrix)
    return matrix


def twice(matrix, axis):
    matrix = matrix.astype(BF16)
    return jnp.concatenate((matrix, matrix), axis=axis)


def dot(a, b):
    return jnp.dot(a, b, preferred_element_type=F32)


def rows_of(blocks):
    return jnp.concatenate(blocks, axis=0)


def columns_of(blocks):
    return jnp.concatenate(blocks, axis=1)


def kernel(
    doms, cells,
    kappa_hbm, source_hbm, adjoint_hbm, wave, residual, cell, receiver, out,
    kappa, given, fields, totals, part, spot, marks, row_side, column_side, inject_side,
    blur_row, blur_column, order,
    first_in, second_out, second_in, y_out, y_in, y_sum, power_out, power_in,
    load_sem, halo_send, halo_recv,
    first_send, first_recv, second_send, second_recv, y_send, y_recv, p_send, p_recv,
):
    depth, width, span = kappa.shape
    shot, dom = lax.axis_index("shot"), lax.axis_index("dom")
    core = dom % 2
    anchor = dom * depth
    parts_y, parts_x, parts_z = SHOT_PARTS
    rows = width // (parts_y * parts_x * parts_z)
    z_at, x_at, y_at = shot % parts_z, shot // parts_z % parts_x, shot // (parts_z * parts_x)
    first_two = ((parts_x, parts_z), (parts_z, parts_x))

    def by_x(step):
        return ((y_at * parts_x + (x_at + step) % parts_x) * parts_z + z_at, dom)

    def by_z(step):
        return ((y_at * parts_x + x_at) * parts_z + (z_at + step) % parts_z, dom)

    def by_y(step):
        return (((y_at + step) % parts_y * parts_x + x_at) * parts_z + z_at, dom)

    def by_dom(step):
        return (shot, (dom + step) % doms)

    loads = []
    for at, (source, target) in enumerate(
        (
            (source_hbm.at[0], given[0][0]),
            (adjoint_hbm.at[0], given[1][0]),
            (kappa_hbm, kappa),
            (source_hbm.at[1], given[0][1]),
            (adjoint_hbm.at[1], given[1][1]),
        )
    ):
        copy = pltpu.make_async_copy(source, target, load_sem.at[at])
        copy.start()
        loads.append(copy)

    barrier = pltpu.get_barrier_semaphore()
    stages = (
        [by_dom(step) for step in range(1, doms)],
        [by_z(step) for step in range(1, parts_z)],
        [by_x(step) for step in range(1, parts_x)],
    )
    peers = [peer for stage in stages for peer in stage]
    peers += [by_y(step) for step in range(1, parts_y)]
    for peer in peers:
        pl.semaphore_signal(barrier, inc=1, device_id=peer, device_id_type=MESH)

    @pl.when(dom == 0)
    def _():
        for which in (0, 1):
            for level in range(LEVELS):
                fields[which][level][0:HALO] = jnp.zeros((HALO, width, span), F32)

    @pl.when(dom == doms - 1)
    def _():
        for which in (0, 1):
            for level in range(LEVELS):
                fields[which][level][HALO + depth :] = jnp.zeros((HALO, width, span), F32)

    def beside(side):
        neighbour = dom + 2 * side - 1
        return neighbour, (neighbour >= 0) & (neighbour < doms)

    def halo_copy(which, level, side, landing):
        field = fields[which][level]
        return pltpu.make_async_remote_copy(
            src_ref=field.at[pl.ds(HALO + (depth - HALO) * side, HALO)],
            dst_ref=field.at[pl.ds((HALO + depth) * landing, HALO)],
            send_sem=halo_send.at[which, level, side],
            recv_sem=halo_recv.at[which, level, landing],
            device_id=(shot, beside(side)[0]),
            device_id_type=MESH,
        )

    def halo_start(which, level, side):
        @pl.when(beside(side)[1])
        def _():
            halo_copy(which, level, side, 1 - side).start()

    def halo_wait(which, level, side):
        @pl.when(beside(side)[1])
        def _():
            halo_copy(which, level, side, side).wait_recv()

    for which in (0, 1):
        loads[which].wait()
        field = fields[which][LEVELS - 1]
        for start in (0, depth - HALO):
            field[start + HALO : start + 2 * HALO] = given[which][0][
                start : start + HALO
            ].astype(F32)
        if which == 0:
            pl.semaphore_wait(barrier, len(peers))
        for turn in (0, 1):
            halo_start(which, LEVELS - 1, turn ^ core)
    for which in (0, 1):
        fields[which][LEVELS - 1][2 * HALO : depth] = given[which][0][
            HALO : depth - HALO
        ].astype(F32)

    row_side[...] = twice(band(width, (0.0,) + RING), 1)
    column_side[...] = twice(band(span, (0.0,) + RING), 0)
    first = lax.broadcasted_iota(jnp.int32, (width, span), 0) == cell[1]
    second = lax.broadcasted_iota(jnp.int32, (width, span), 1) == cell[2]
    spot[...] = jnp.where(first & second, 1.0, 0.0)
    lines = lax.broadcasted_iota(jnp.int32, (span, receiver.shape[2]), 0)
    for level in range(1, LEVELS):
        spread = jnp.where(lines == receiver[2], residual[level : level + 1, :], 0.0)
        inject_side[level] = columns_of(split(jnp.transpose(spread)))
    lines = lax.broadcasted_iota(jnp.int32, (width, receiver.shape[2]), 0)

    @pl.loop(0, depth)
    def _(z):
        hit = (lines == receiver[1]) & (receiver[0] == anchor + z)
        marks[z] = jnp.where(hit, 1.0, 0.0).astype(BF16)

    place = lax.broadcasted_iota(jnp.int32, (width, width), 0)
    row = place % rows
    y_hi = place // rows % parts_y
    for way, parts in enumerate(first_two):
        minor = place // (rows * parts_y) % parts[1]
        major = place // (rows * parts_y * parts[1])
        x_of, z_of = (major, minor) if way == 0 else (minor, major)
        wanted = ((y_hi * parts_x + x_of) * parts_z + z_of) * rows + row
        distance = jnp.abs(wanted - lax.broadcasted_iota(jnp.int32, (width, width), 1))
        taps = jnp.zeros((width, width), F32)
        for d, weight in enumerate((0.375, 0.25, 0.0625)):
            taps = jnp.where(distance == d, weight, taps)
        blur_row[way] = twice(taps, 1)
    blur_column[...] = twice(band(span, (0.375, 0.25, 0.0625)), 0)
    for way, parts in enumerate(first_two):
        count = HALO * width // parts[0]
        place = lax.broadcasted_iota(jnp.int32, (count, count), 0)
        row = place % rows
        layer = place // rows % HALO
        y_hi = place // (rows * HALO) % parts_y
        minor = place // (rows * HALO * parts_y)
        wanted = ((layer * parts[1] + minor) * parts_y + y_hi) * rows + row
        hit = wanted == lax.broadcasted_iota(jnp.int32, (count, count), 1)
        order[way][...] = twice(jnp.where(hit, 1.0, 0.0), 1)

    def both_sides(blocks, left, right):
        flat = rows_of([columns_of(block) for block in blocks])
        upright = columns_of([rows_of(block) for block in blocks])
        flat, upright = dot(flat, right), dot(left, upright)
        return [
            flat[at * width : (at + 1) * width] + upright[:, at * span : (at + 1) * span]
            for at in range(len(blocks))
        ]

    def advance(which, level, start):
        field = fields[which][level]
        layers = range(HALO)
        if level == LEVELS - 1:
            blocks = [(given[which][0][start + at],) for at in layers]
            lateral = both_sides(blocks, row_side[:, :width], column_side[:span])
        else:
            blocks = [split(field[start + at + HALO]) for at in layers]
            lateral = both_sides(blocks, row_side[...], column_side[...])
        if which == 1:
            inject = dot(rows_of([marks[start + at] for at in layers]), inject_side[level])
            inject = inject[:, :span] + inject[:, span:]
            inject = [inject[at * width : (at + 1) * width] for at in layers]
        else:
            inject = [
                jnp.where(cell[0] == anchor + start + at, wave[level], 0.0) * spot[...]
                for at in layers
            ]
        blurred = []
        for at in layers:
            z = start + at
            current = field[z + HALO]
            summed = lateral[at] + CENTER * current
            for shift in range(1, HALO + 1):
                summed = summed + RING[shift - 1] * (
                    field[z + HALO + shift] + field[z + HALO - shift]
                )
            term = kappa[z] * (summed * (1.0 / SCALE)) + inject[at]
            if which == 0:
                product = fields[1][level][z + HALO] * term
                if level < LEVELS - 1:
                    product = product + totals[level][z]
                if level > 0:
                    totals[level - 1][z] = product
                else:
                    blurred.append(product)
            if level > 0:
                if level == LEVELS - 1:
                    later = given[which][1][z].astype(F32)
                else:
                    later = fields[which][level + 1][z + HALO]
                fields[which][level - 1][z + HALO] = 2.0 * current - later + term
        return blurred

    def blur(blurred, start, way):
        flat = dot(rows_of([columns_of(split(at)) for at in blurred]), blur_column[...])
        blocks = [flat[at * width : (at + 1) * width] for at in range(HALO)]
        upright = dot(blur_row[way], columns_of([rows_of(split(at)) for at in blocks]))
        for at in range(HALO):
            part[start + at] = upright[:, at * span : (at + 1) * span]

    def remote(source, target, send_sem, recv_sem, peer):
        return pltpu.make_async_remote_copy(
            src_ref=source,
            dst_ref=target,
            send_sem=send_sem,
            recv_sem=recv_sem,
            device_id=peer,
            device_id_type=MESH,
        )

    inner, outer = (depth - HALO) * (1 - core), (depth - HALO) * core
    starts = (HALO, 2 * HALO, inner, outer)
    ways = (1, 0, 0, 0)
    spots = (x_at, z_at)

    def first_copy(chunk, step):
        way = ways[chunk]
        stripe = width // first_two[way][0]
        place = (spots[way] + step) % first_two[way][0] * stripe
        return remote(
            part.at[pl.ds(starts[chunk], HALO), pl.ds(pl.multiple_of(place, stripe), stripe)],
            first_in[way].at[max(chunk - 1, 0), step - 1],
            first_send.at[chunk, step - 1],
            first_recv.at[chunk, step - 1],
            (by_x, by_z)[way](step),
        )

    def second_copy(chunk, step):
        way = ways[chunk]
        return remote(
            second_out[way].at[max(chunk - 1, 0), (spots[1 - way] + step) % first_two[way][1]],
            second_in[way].at[max(chunk - 1, 0), step - 1],
            second_send.at[chunk, step - 1],
            second_recv.at[chunk, step - 1],
            (by_z, by_x)[way](step),
        )

    def y_copy(chunk, step):
        return remote(
            y_out.at[chunk],
            y_in.at[chunk, step - 1],
            y_send.at[chunk, step - 1],
            y_recv.at[chunk, step - 1],
            by_y(step),
        )

    def first_steps(chunk):
        return range(1, first_two[ways[chunk]][0])

    def second_steps(chunk):
        return range(1, first_two[ways[chunk]][1])

    def finish(chunk):
        start = starts[chunk]
        blur(advance(0, 0, start), start, ways[chunk])
        for step in first_steps(chunk):
            first_copy(chunk, step).start()

    def inside(which, level):
        @pl.loop(HALO, depth - HALO, step=HALO)
        def _(start):
            advance(which, level, start)

    def sides(which, level):
        @pl.loop(0, 2)
        def _(turn):
            side = turn ^ core
            halo_wait(which, level, side)
            advance(which, level, (depth - HALO) * side)
            if level > 1 or which == 0:
                halo_start(which, level - 1, side)

    for load in loads[2:]:
        load.wait()
    for which in (0, 1):
        inside(which, LEVELS - 1)
    for which in (0, 1):
        sides(which, LEVELS - 1)
    for level in reversed(range(2, LEVELS - 1)):
        for which in (0, 1):
            sides(which, level)
            inside(which, level)
    sides(0, 1)
    inside(0, 1)
    inside(1, 1)
    finish(0)
    finish(1)
    for chunk, side in ((2, 1 - core), (3, core)):
        halo_wait(1, 1, side)
        advance(1, 1, starts[chunk])
        halo_wait(0, 0, side)
        finish(chunk)

    for chunk in (1, 2, 0, 3):
        way = ways[chunk]
        parts = first_two[way]
        stripe = width // parts[0]
        own = pl.multiple_of(spots[way] * stripe, stripe)
        summed = part[pl.ds(starts[chunk], HALO), pl.ds(own, stripe)]
        for step in first_steps(chunk):
            first_copy(chunk, step).wait_recv()
            summed = summed + first_in[way][max(chunk - 1, 0), step - 1]
        moved = dot(order[way][...], rows_of(split(summed.reshape(HALO * stripe, span))))
        second_out[way][max(chunk - 1, 0)] = moved.reshape(parts[1], HALO * stripe // parts[1], span)
        for step in second_steps(chunk):
            second_copy(chunk, step).start()
    block = rows * HALO
    for chunk in (1, 2, 0, 3):
        way = ways[chunk]
        summed = second_out[way][max(chunk - 1, 0), spots[1 - way]]
        for step in second_steps(chunk):
            second_copy(chunk, step).wait_recv()
            summed = summed + second_in[way][max(chunk - 1, 0), step - 1]
        y_out[chunk] = summed.reshape(parts_y, block, span)
        for step in range(1, parts_y):
            y_copy(chunk, step).start()
    power = jnp.zeros((block, span), F32)
    for chunk in (1, 2, 0, 3):
        summed = y_out[chunk]
        for step in range(1, parts_y):
            y_copy(chunk, step).wait_recv()
            summed = summed + y_in[chunk, step - 1]
        y_sum[chunk] = summed
        for y_hi in range(parts_y):
            power = power + summed[y_hi] * summed[y_hi]
    power_copies = []
    for stage, peers in enumerate(stages):
        power_out[stage] = power
        now = [
            remote(
                power_out.at[stage],
                power_in.at[stage, step],
                p_send.at[stage, step],
                p_recv.at[stage, step],
                peer,
            )
            for step, peer in enumerate(peers)
        ]
        for copy in now:
            copy.start()
        for step, copy in enumerate(now):
            copy.wait_recv()
            power = power + power_in[stage, step]
        power_copies += now
    scale = lax.rsqrt(jnp.full((1, 1), jnp.sum(power)) * (1.0 / cells) + 1e-6)
    for chunk, start in enumerate(starts):
        place = start * rows
        if not isinstance(place, int):
            place = pl.multiple_of(place, block)
        out[pl.ds(place, block)] = -y_sum[chunk, y_at] * scale

    for chunk in range(len(starts)):
        for step in first_steps(chunk):
            first_copy(chunk, step).wait_send()
        for step in second_steps(chunk):
            second_copy(chunk, step).wait_send()
        for step in range(1, parts_y):
            y_copy(chunk, step).wait_send()
    for copy in power_copies:
        copy.wait_send()
    for level in reversed(range(LEVELS)):
        for which in (0, 1) if level > 0 else (0,):
            for side in (0, 1):

                @pl.when(beside(side)[1])
                def _():
                    halo_copy(which, level, side, 1 - side).wait_send()


def per_device(doms, kappa, source_pair, adjoint_pair, wavelet, residuals, source_cell, receiver_cells):
    depth, width, span = kappa.shape
    receivers = receiver_cells.shape[2]
    parts_y, parts_x, parts_z = SHOT_PARTS
    rows = width // (parts_y * parts_x * parts_z)
    chunks = depth // HALO
    counts = (HALO * width // parts_x, HALO * width // parts_z)
    block = rows * HALO
    most = max(doms, parts_z, parts_x) - 1
    hbm = pl.BlockSpec(memory_space=pl.ANY)
    vmem = pl.BlockSpec(memory_space=pltpu.VMEM)
    smem = pl.BlockSpec(memory_space=pltpu.SMEM)
    dma = pltpu.SemaphoreType.DMA
    slab = pltpu.VMEM(kappa.shape, F32)
    padded = pltpu.VMEM((depth + 2 * HALO, width, span), F32)
    first = pltpu.VMEM(kappa.shape, BF16)
    direction = pl.pallas_call(
        functools.partial(kernel, doms, float(depth * doms * width * span)),
        out_shape=jax.ShapeDtypeStruct((depth * rows, span), F32),
        in_specs=[hbm, hbm, hbm, smem, vmem, smem, vmem],
        out_specs=vmem,
        scratch_shapes=[
            slab,
            [[first] * 2] * 2,
            [[padded] * LEVELS] * 2,
            [slab] * (LEVELS - 1),
            slab,
            pltpu.VMEM((width, span), F32),
            pltpu.VMEM((depth, width, receivers), BF16),
            pltpu.VMEM((width, 2 * width), BF16),
            pltpu.VMEM((2 * span, span), BF16),
            pltpu.VMEM((LEVELS, receivers, 2 * span), BF16),
            pltpu.VMEM((2, width, 2 * width), BF16),
            pltpu.VMEM((2 * span, span), BF16),
            [pltpu.VMEM((count, 2 * count), BF16) for count in counts],
            [
                pltpu.VMEM((most, parts - 1, HALO, width // parts, span), F32)
                for most, parts in ((chunks - 1, parts_x), (1, parts_z))
            ],
            [
                pltpu.VMEM((most, parts, block * parts_y, span), F32)
                for most, parts in ((chunks - 1, parts_z), (1, parts_x))
            ],
            [
                pltpu.VMEM((most, parts - 1, block * parts_y, span), F32)
                for most, parts in ((chunks - 1, parts_z), (1, parts_x))
            ],
            pltpu.VMEM((chunks, parts_y, block, span), F32),
            pltpu.VMEM((chunks, parts_y - 1, parts_y, block, span), F32),
            pltpu.VMEM((chunks, parts_y, block, span), F32),
            pltpu.VMEM((3, block, span), F32),
            pltpu.VMEM((3, most, block, span), F32),
            dma((5,)),
            dma((2, LEVELS, 2)),
            dma((2, LEVELS, 2)),
            dma((chunks, most)),
            dma((chunks, most)),
            dma((chunks, most)),
            dma((chunks, most)),
            dma((chunks, parts_y - 1)),
            dma((chunks, parts_y - 1)),
            dma((3, most)),
            dma((3, most)),
        ],
        compiler_params=pltpu.CompilerParams(
            collective_id=0, has_side_effects=True, vmem_limit_bytes=56164352
        ),
    )(
        kappa,
        source_pair[0],
        adjoint_pair[0],
        wavelet[0],
        residuals[0],
        source_cell[0],
        jnp.transpose(receiver_cells, (1, 0, 2)),
    )
    return direction.reshape(depth, rows, span)


def solution(mesh):
    return jax.shard_map(
        functools.partial(per_device, mesh.shape["dom"]),
        mesh=mesh,
        in_specs=(
            P("dom", None, None),
            P("shot", None, "dom", None, None),
            P("shot", None, "dom", None, None),
            P("shot", None),
            P("shot", None, None),
            P("shot", None),
            P("shot", None, None),
        ),
        out_specs=P("dom", "shot", None),
        check_vma=False,
    )
```

```python
import functools

import jax
import jax.numpy as jnp
from jax import lax
from jax.experimental import pallas as pl
from jax.experimental.pallas import tpu as pltpu
from jax.sharding import PartitionSpec as P

MESH = pl.DeviceIdType.MESH
LEVELS = 4
HALO = 4
SCALE = 5040.0
RING = (8064.0, -1008.0, 128.0, -9.0)
CENTER = 3.0 * -14350.0
SHOT_PARTS = (2, 4, 8)
F32 = jnp.float32
BF16 = jnp.bfloat16


def split(value):
    high = value.astype(BF16)
    low = (value - high.astype(F32)).astype(BF16)
    return high, low


def band(size, weights):
    rows = lax.broadcasted_iota(jnp.int32, (size, size), 0)
    columns = lax.broadcasted_iota(jnp.int32, (size, size), 1)
    distance = jnp.abs(rows - columns)
    matrix = jnp.zeros((size, size), F32)
    for d, weight in enumerate(weights):
        matrix = jnp.where(distance == d, weight, matrix)
    return matrix


def twice(matrix, axis):
    matrix = matrix.astype(BF16)
    return jnp.concatenate((matrix, matrix), axis=axis)


def dot(a, b):
    return jnp.dot(a, b, preferred_element_type=F32)


def rows_of(blocks):
    return jnp.concatenate(blocks, axis=0)


def columns_of(blocks):
    return jnp.concatenate(blocks, axis=1)


def kernel(
    doms, cells,
    kappa_hbm, source_hbm, adjoint_hbm, wave, residual, cell, receiver, out,
    kappa, given, fields, totals, part, spot, marks, row_side, column_side, inject_side,
    blur_row, blur_column, order,
    first_in, second_out, second_in, y_out, y_in, y_sum, power_out, power_in,
    load_sem, halo_send, halo_recv,
    first_send, first_recv, second_send, second_recv, y_send, y_recv, p_send, p_recv,
):
    depth, width, span = kappa.shape
    shot, dom = lax.axis_index("shot"), lax.axis_index("dom")
    core = dom % 2
    anchor = dom * depth
    parts_y, parts_x, parts_z = SHOT_PARTS
    rows = width // (parts_y * parts_x * parts_z)
    z_at, x_at, y_at = shot % parts_z, shot // parts_z % parts_x, shot // (parts_z * parts_x)
    first_two = ((parts_x, parts_z), (parts_z, parts_x))

    def by_x(step):
        return ((y_at * parts_x + (x_at + step) % parts_x) * parts_z + z_at, dom)

    def by_z(step):
        return ((y_at * parts_x + x_at) * parts_z + (z_at + step) % parts_z, dom)

    def by_y(step):
        return (((y_at + step) % parts_y * parts_x + x_at) * parts_z + z_at, dom)

    def by_dom(step):
        return (shot, (dom + step) % doms)

    loads = []
    for at, (source, target) in enumerate(
        (
            (source_hbm.at[0], given[0][0]),
            (adjoint_hbm.at[0], given[1][0]),
            (kappa_hbm, kappa),
            (source_hbm.at[1], given[0][1]),
            (adjoint_hbm.at[1], given[1][1]),
        )
    ):
        copy = pltpu.make_async_copy(source, target, load_sem.at[at])
        copy.start()
        loads.append(copy)

    barrier = pltpu.get_barrier_semaphore()
    stages = (
        [by_dom(step) for step in range(1, doms)],
        [by_z(step) for step in range(1, parts_z)],
        [by_x(step) for step in range(1, parts_x)],
    )
    peers = [peer for stage in stages for peer in stage]
    peers += [by_y(step) for step in range(1, parts_y)]
    for peer in peers:
        pl.semaphore_signal(barrier, inc=1, device_id=peer, device_id_type=MESH)

    @pl.when(dom == 0)
    def _():
        for which in (0, 1):
            for level in range(LEVELS):
                fields[which][level][0:HALO] = jnp.zeros((HALO, width, span), F32)

    @pl.when(dom == doms - 1)
    def _():
        for which in (0, 1):
            for level in range(LEVELS):
                fields[which][level][HALO + depth :] = jnp.zeros((HALO, width, span), F32)

    def beside(side):
        neighbour = dom + 2 * side - 1
        return neighbour, (neighbour >= 0) & (neighbour < doms)

    def halo_copy(which, level, side, landing):
        field = fields[which][level]
        return pltpu.make_async_remote_copy(
            src_ref=field.at[pl.ds(HALO + (depth - HALO) * side, HALO)],
            dst_ref=field.at[pl.ds((HALO + depth) * landing, HALO)],
            send_sem=halo_send.at[which, level, side],
            recv_sem=halo_recv.at[which, level, landing],
            device_id=(shot, beside(side)[0]),
            device_id_type=MESH,
        )

    def halo_start(which, level, side):
        @pl.when(beside(side)[1])
        def _():
            halo_copy(which, level, side, 1 - side).start()

    def halo_wait(which, level, side):
        @pl.when(beside(side)[1])
        def _():
            halo_copy(which, level, side, side).wait_recv()

    for which in (0, 1):
        loads[which].wait()
        field = fields[which][LEVELS - 1]
        for start in (0, depth - HALO):
            field[start + HALO : start + 2 * HALO] = given[which][0][
                start : start + HALO
            ].astype(F32)
        if which == 0:
            pl.semaphore_wait(barrier, len(peers))
        for turn in (0, 1):
            halo_start(which, LEVELS - 1, turn ^ core)
    for which in (0, 1):
        fields[which][LEVELS - 1][2 * HALO : depth] = given[which][0][
            HALO : depth - HALO
        ].astype(F32)

    row_side[...] = twice(band(width, (0.0,) + RING), 1)
    column_side[...] = twice(band(span, (0.0,) + RING), 0)
    first = lax.broadcasted_iota(jnp.int32, (width, span), 0) == cell[1]
    second = lax.broadcasted_iota(jnp.int32, (width, span), 1) == cell[2]
    spot[...] = jnp.where(first & second, 1.0, 0.0)
    lines = lax.broadcasted_iota(jnp.int32, (span, receiver.shape[2]), 0)
    for level in range(1, LEVELS):
        spread = jnp.where(lines == receiver[2], residual[level : level + 1, :], 0.0)
        inject_side[level] = columns_of(split(jnp.transpose(spread)))
    lines = lax.broadcasted_iota(jnp.int32, (width, receiver.shape[2]), 0)

    @pl.loop(0, depth)
    def _(z):
        hit = (lines == receiver[1]) & (receiver[0] == anchor + z)
        marks[z] = jnp.where(hit, 1.0, 0.0).astype(BF16)

    place = lax.broadcasted_iota(jnp.int32, (width, width), 0)
    row = place % rows
    y_hi = place // rows % parts_y
    for way, parts in enumerate(first_two):
        minor = place // (rows * parts_y) % parts[1]
        major = place // (rows * parts_y * parts[1])
        x_of, z_of = (major, minor) if way == 0 else (minor, major)
        wanted = ((y_hi * parts_x + x_of) * parts_z + z_of) * rows + row
        distance = jnp.abs(wanted - lax.broadcasted_iota(jnp.int32, (width, width), 1))
        taps = jnp.zeros((width, width), F32)
        for d, weight in enumerate((0.375, 0.25, 0.0625)):
            taps = jnp.where(distance == d, weight, taps)
        blur_row[way] = twice(taps, 1)
    blur_column[...] = twice(band(span, (0.375, 0.25, 0.0625)), 0)
    for way, parts in enumerate(first_two):
        count = HALO * width // parts[0]
        place = lax.broadcasted_iota(jnp.int32, (count, count), 0)
        row = place % rows
        layer = place // rows % HALO
        y_hi = place // (rows * HALO) % parts_y
        minor = place // (rows * HALO * parts_y)
        wanted = ((layer * parts[1] + minor) * parts_y + y_hi) * rows + row
        hit = wanted == lax.broadcasted_iota(jnp.int32, (count, count), 1)
        order[way][...] = twice(jnp.where(hit, 1.0, 0.0), 1)

    def both_sides(blocks, left, right):
        flat = rows_of([columns_of(block) for block in blocks])
        upright = columns_of([rows_of(block) for block in blocks])
        flat, upright = dot(flat, right), dot(left, upright)
        return [
            flat[at * width : (at + 1) * width] + upright[:, at * span : (at + 1) * span]
            for at in range(len(blocks))
        ]

    def advance(which, level, start):
        field = fields[which][level]
        layers = range(HALO)
        if level == LEVELS - 1:
            blocks = [(given[which][0][start + at],) for at in layers]
            lateral = both_sides(blocks, row_side[:, :width], column_side[:span])
        else:
            blocks = [split(field[start + at + HALO]) for at in layers]
            lateral = both_sides(blocks, row_side[...], column_side[...])
        if which == 1:
            inject = dot(rows_of([marks[start + at] for at in layers]), inject_side[level])
            inject = inject[:, :span] + inject[:, span:]
            inject = [inject[at * width : (at + 1) * width] for at in layers]
        else:
            inject = [
                jnp.where(cell[0] == anchor + start + at, wave[level], 0.0) * spot[...]
                for at in layers
            ]
        blurred = []
        for at in layers:
            z = start + at
            current = field[z + HALO]
            summed = lateral[at] + CENTER * current
            for shift in range(1, HALO + 1):
                summed = summed + RING[shift - 1] * (
                    field[z + HALO + shift] + field[z + HALO - shift]
                )
            term = kappa[z] * (summed * (1.0 / SCALE)) + inject[at]
            if which == 0:
                product = fields[1][level][z + HALO] * term
                if level < LEVELS - 1:
                    product = product + totals[level][z]
                if level > 0:
                    totals[level - 1][z] = product
                else:
                    blurred.append(product)
            if level > 0:
                if level == LEVELS - 1:
                    later = given[which][1][z].astype(F32)
                else:
                    later = fields[which][level + 1][z + HALO]
                fields[which][level - 1][z + HALO] = 2.0 * current - later + term
        return blurred

    def blur(blurred, start, way):
        flat = dot(rows_of([columns_of(split(at)) for at in blurred]), blur_column[...])
        blocks = [flat[at * width : (at + 1) * width] for at in range(HALO)]
        upright = dot(blur_row[way], columns_of([rows_of(split(at)) for at in blocks]))
        for at in range(HALO):
            part[start + at] = upright[:, at * span : (at + 1) * span]

    def remote(source, target, send_sem, recv_sem, peer):
        return pltpu.make_async_remote_copy(
            src_ref=source,
            dst_ref=target,
            send_sem=send_sem,
            recv_sem=recv_sem,
            device_id=peer,
            device_id_type=MESH,
        )

    inner, outer = (depth - HALO) * (1 - core), (depth - HALO) * core
    starts = (HALO, 2 * HALO, inner, outer)
    ways = (1, 0, 0, 0)
    spots = (x_at, z_at)

    def first_copy(chunk, step):
        way = ways[chunk]
        stripe = width // first_two[way][0]
        place = (spots[way] + step) % first_two[way][0] * stripe
        return remote(
            part.at[pl.ds(starts[chunk], HALO), pl.ds(pl.multiple_of(place, stripe), stripe)],
            first_in[way].at[max(chunk - 1, 0), step - 1],
            first_send.at[chunk, step - 1],
            first_recv.at[chunk, step - 1],
            (by_x, by_z)[way](step),
        )

    def second_copy(chunk, step):
        way = ways[chunk]
        return remote(
            second_out[way].at[max(chunk - 1, 0), (spots[1 - way] + step) % first_two[way][1]],
            second_in[way].at[max(chunk - 1, 0), step - 1],
            second_send.at[chunk, step - 1],
            second_recv.at[chunk, step - 1],
            (by_z, by_x)[way](step),
        )

    def y_copy(chunk, step):
        return remote(
            y_out.at[chunk],
            y_in.at[chunk, step - 1],
            y_send.at[chunk, step - 1],
            y_recv.at[chunk, step - 1],
            by_y(step),
        )

    def first_steps(chunk):
        return range(1, first_two[ways[chunk]][0])

    def second_steps(chunk):
        return range(1, first_two[ways[chunk]][1])

    def finish(chunk):
        start = starts[chunk]
        blur(advance(0, 0, start), start, ways[chunk])
        for step in first_steps(chunk):
            first_copy(chunk, step).start()

    def inside(which, level):
        @pl.loop(HALO, depth - HALO, step=HALO)
        def _(start):
            advance(which, level, start)

    def sides(which, level):
        @pl.loop(0, 2)
        def _(turn):
            side = turn ^ core
            halo_wait(which, level, side)
            advance(which, level, (depth - HALO) * side)
            if level > 1 or which == 0:
                halo_start(which, level - 1, side)

    for load in loads[2:]:
        load.wait()
    for level in reversed(range(2, LEVELS)):
        for which in (0, 1):
            inside(which, level)
            sides(which, level)
    inside(0, 1)
    inside(1, 1)
    sides(0, 1)
    finish(1)
    finish(0)
    for chunk, side in ((2, 1 - core), (3, core)):
        halo_wait(1, 1, side)
        advance(1, 1, starts[chunk])
        halo_wait(0, 0, side)
        finish(chunk)

    for chunk in (1, 2, 0, 3):
        way = ways[chunk]
        parts = first_two[way]
        stripe = width // parts[0]
        own = pl.multiple_of(spots[way] * stripe, stripe)
        summed = part[pl.ds(starts[chunk], HALO), pl.ds(own, stripe)]
        for step in first_steps(chunk):
            first_copy(chunk, step).wait_recv()
            summed = summed + first_in[way][max(chunk - 1, 0), step - 1]
        moved = dot(order[way][...], rows_of(split(summed.reshape(HALO * stripe, span))))
        second_out[way][max(chunk - 1, 0)] = moved.reshape(parts[1], HALO * stripe // parts[1], span)
        for step in second_steps(chunk):
            second_copy(chunk, step).start()
    block = rows * HALO
    for chunk in (1, 2, 0, 3):
        way = ways[chunk]
        summed = second_out[way][max(chunk - 1, 0), spots[1 - way]]
        for step in second_steps(chunk):
            second_copy(chunk, step).wait_recv()
            summed = summed + second_in[way][max(chunk - 1, 0), step - 1]
        y_out[chunk] = summed.reshape(parts_y, block, span)
        for step in range(1, parts_y):
            y_copy(chunk, step).start()
    power = jnp.zeros((block, span), F32)
    for chunk in (1, 2, 0, 3):
        summed = y_out[chunk]
        for step in range(1, parts_y):
            y_copy(chunk, step).wait_recv()
            summed = summed + y_in[chunk, step - 1]
        y_sum[chunk] = summed
        for y_hi in range(parts_y):
            power = power + summed[y_hi] * summed[y_hi]
    power_copies = []
    for stage, peers in enumerate(stages):
        power_out[stage] = power
        now = [
            remote(
                power_out.at[stage],
                power_in.at[stage, step],
                p_send.at[stage, step],
                p_recv.at[stage, step],
                peer,
            )
            for step, peer in enumerate(peers)
        ]
        for copy in now:
            copy.start()
        for step, copy in enumerate(now):
            copy.wait_recv()
            power = power + power_in[stage, step]
        power_copies += now
    scale = lax.rsqrt(jnp.full((1, 1), jnp.sum(power)) * (1.0 / cells) + 1e-6)
    for chunk, start in enumerate(starts):
        place = start * rows
        if not isinstance(place, int):
            place = pl.multiple_of(place, block)
        out[pl.ds(place, block)] = -y_sum[chunk, y_at] * scale

    for chunk in range(len(starts)):
        for step in first_steps(chunk):
            first_copy(chunk, step).wait_send()
        for step in second_steps(chunk):
            second_copy(chunk, step).wait_send()
        for step in range(1, parts_y):
            y_copy(chunk, step).wait_send()
    for copy in power_copies:
        copy.wait_send()
    for level in reversed(range(LEVELS)):
        for which in (0, 1) if level > 0 else (0,):
            for side in (0, 1):

                @pl.when(beside(side)[1])
                def _():
                    halo_copy(which, level, side, 1 - side).wait_send()


def per_device(doms, kappa, source_pair, adjoint_pair, wavelet, residuals, source_cell, receiver_cells):
    depth, width, span = kappa.shape
    receivers = receiver_cells.shape[2]
    parts_y, parts_x, parts_z = SHOT_PARTS
    rows = width // (parts_y * parts_x * parts_z)
    chunks = depth // HALO
    counts = (HALO * width // parts_x, HALO * width // parts_z)
    block = rows * HALO
    most = max(doms, parts_z, parts_x) - 1
    hbm = pl.BlockSpec(memory_space=pl.ANY)
    vmem = pl.BlockSpec(memory_space=pltpu.VMEM)
    smem = pl.BlockSpec(memory_space=pltpu.SMEM)
    dma = pltpu.SemaphoreType.DMA
    slab = pltpu.VMEM(kappa.shape, F32)
    padded = pltpu.VMEM((depth + 2 * HALO, width, span), F32)
    first = pltpu.VMEM(kappa.shape, BF16)
    direction = pl.pallas_call(
        functools.partial(kernel, doms, float(depth * doms * width * span)),
        out_shape=jax.ShapeDtypeStruct((depth * rows, span), F32),
        in_specs=[hbm, hbm, hbm, smem, vmem, smem, vmem],
        out_specs=vmem,
        scratch_shapes=[
            slab,
            [[first] * 2] * 2,
            [[padded] * LEVELS] * 2,
            [slab] * (LEVELS - 1),
            slab,
            pltpu.VMEM((width, span), F32),
            pltpu.VMEM((depth, width, receivers), BF16),
            pltpu.VMEM((width, 2 * width), BF16),
            pltpu.VMEM((2 * span, span), BF16),
            pltpu.VMEM((LEVELS, receivers, 2 * span), BF16),
            pltpu.VMEM((2, width, 2 * width), BF16),
            pltpu.VMEM((2 * span, span), BF16),
            [pltpu.VMEM((count, 2 * count), BF16) for count in counts],
            [
                pltpu.VMEM((most, parts - 1, HALO, width // parts, span), F32)
                for most, parts in ((chunks - 1, parts_x), (1, parts_z))
            ],
            [
                pltpu.VMEM((most, parts, block * parts_y, span), F32)
                for most, parts in ((chunks - 1, parts_z), (1, parts_x))
            ],
            [
                pltpu.VMEM((most, parts - 1, block * parts_y, span), F32)
                for most, parts in ((chunks - 1, parts_z), (1, parts_x))
            ],
            pltpu.VMEM((chunks, parts_y, block, span), F32),
            pltpu.VMEM((chunks, parts_y - 1, parts_y, block, span), F32),
            pltpu.VMEM((chunks, parts_y, block, span), F32),
            pltpu.VMEM((3, block, span), F32),
            pltpu.VMEM((3, most, block, span), F32),
            dma((5,)),
            dma((2, LEVELS, 2)),
            dma((2, LEVELS, 2)),
            dma((chunks, most)),
            dma((chunks, most)),
            dma((chunks, most)),
            dma((chunks, most)),
            dma((chunks, parts_y - 1)),
            dma((chunks, parts_y - 1)),
            dma((3, most)),
            dma((3, most)),
        ],
        compiler_params=pltpu.CompilerParams(
            collective_id=0, has_side_effects=True, vmem_limit_bytes=56164352
        ),
    )(
        kappa,
        source_pair[0],
        adjoint_pair[0],
        wavelet[0],
        residuals[0],
        source_cell[0],
        jnp.transpose(receiver_cells, (1, 0, 2)),
    )
    return direction.reshape(depth, rows, span)


def solution(mesh):
    return jax.shard_map(
        functools.partial(per_device, mesh.shape["dom"]),
        mesh=mesh,
        in_specs=(
            P("dom", None, None),
            P("shot", None, "dom", None, None),
            P("shot", None, "dom", None, None),
            P("shot", None),
            P("shot", None, None),
            P("shot", None),
            P("shot", None, None),
        ),
        out_specs=P("dom", "shot", None),
        check_vma=False,
    )
```

```python
import functools

import jax
import jax.numpy as jnp
from jax import lax
from jax.experimental import pallas as pl
from jax.experimental.pallas import tpu as pltpu
from jax.sharding import PartitionSpec as P

MESH = pl.DeviceIdType.MESH
LEVELS = 4
HALO = 4
SCALE = 5040.0
RING = (8064.0, -1008.0, 128.0, -9.0)
CENTER = 3.0 * -14350.0
SHOT_PARTS = (2, 4, 8)
F32 = jnp.float32
BF16 = jnp.bfloat16


def split(value):
    high = value.astype(BF16)
    low = (value - high.astype(F32)).astype(BF16)
    return high, low


def band(size, weights):
    rows = lax.broadcasted_iota(jnp.int32, (size, size), 0)
    columns = lax.broadcasted_iota(jnp.int32, (size, size), 1)
    distance = jnp.abs(rows - columns)
    matrix = jnp.zeros((size, size), F32)
    for d, weight in enumerate(weights):
        matrix = jnp.where(distance == d, weight, matrix)
    return matrix


def twice(matrix, axis):
    matrix = matrix.astype(BF16)
    return jnp.concatenate((matrix, matrix), axis=axis)


def dot(a, b):
    return jnp.dot(a, b, preferred_element_type=F32)


def rows_of(blocks):
    return jnp.concatenate(blocks, axis=0)


def columns_of(blocks):
    return jnp.concatenate(blocks, axis=1)


def kernel(
    doms, cells,
    kappa_hbm, source_hbm, adjoint_hbm, wave, residual, cell, receiver, out,
    kappa, given, fields, totals, part, spot, marks, row_side, column_side, inject_side,
    blur_row, blur_column, order,
    first_in, second_out, second_in, y_out, y_in, y_sum, power_out, power_in,
    load_sem, known, halo_send, halo_recv,
    first_send, first_recv, second_send, second_recv, y_send, y_recv, p_send, p_recv,
):
    depth, width, span = kappa.shape
    shot, dom = lax.axis_index("shot"), lax.axis_index("dom")
    core = dom % 2
    anchor = dom * depth
    parts_y, parts_x, parts_z = SHOT_PARTS
    rows = width // (parts_y * parts_x * parts_z)
    z_at, x_at, y_at = shot % parts_z, shot // parts_z % parts_x, shot // (parts_z * parts_x)
    first_two = ((parts_x, parts_z), (parts_z, parts_x))
    ring = parts_y * doms // 2

    def by_x(step):
        return ((y_at * parts_x + (x_at + step) % parts_x) * parts_z + z_at, dom)

    def by_z(step):
        return ((y_at * parts_x + x_at) * parts_z + (z_at + step) % parts_z, dom)

    def by_y(step):
        return (((y_at + step) % parts_y * parts_x + x_at) * parts_z + z_at, dom)

    def by_dom(step):
        return (shot, (dom + step) % doms)

    def by_ring(step, turn):
        at = (y_at * (doms // 2) + dom // 2 + step) % ring
        y_hi, chip = at // (doms // 2), at % (doms // 2)
        return ((y_hi * parts_x + x_at) * parts_z + z_at, chip * 2 + (core + turn) % 2)

    def near(size):
        return sorted({1, size - 1})

    def next_to(size):
        return [2, size - 2] if size > 4 else []

    loads = []
    for at, (source, target) in enumerate(
        (
            (source_hbm.at[0], given[0][0]),
            (adjoint_hbm.at[0], given[1][0]),
            (kappa_hbm, kappa),
            (source_hbm.at[1], given[0][1]),
            (adjoint_hbm.at[1], given[1][1]),
        )
    ):
        copy = pltpu.make_async_copy(source, target, load_sem.at[at])
        copy.start()
        loads.append(copy)

    barrier = pltpu.get_barrier_semaphore()
    stages = (
        [by_dom(step) for step in range(1, doms)],
        [by_z(step) for step in range(1, parts_z)],
        [by_x(step) for step in range(1, parts_x)],
    )
    beyond = [by_ring(step, 0) for step in near(ring)]
    beyond += [by_z(step) for step in near(parts_z)] + [by_x(step) for step in near(parts_x)]
    peers = [by_ring(2 * core - 1, 1), by_ring(0, 1)] + beyond
    farther = [by_ring(step, 0) for step in next_to(ring)]
    farther += [by_z(step) for step in next_to(parts_z)]
    for peer in peers:
        pl.semaphore_signal(barrier, inc=1, device_id=peer, device_id_type=MESH)

    @pl.when(dom == 0)
    def _():
        for which in (0, 1):
            for level in range(LEVELS):
                fields[which][level][0:HALO] = jnp.zeros((HALO, width, span), F32)

    @pl.when(dom == doms - 1)
    def _():
        for which in (0, 1):
            for level in range(LEVELS):
                fields[which][level][HALO + depth :] = jnp.zeros((HALO, width, span), F32)

    def beside(side):
        neighbour = dom + 2 * side - 1
        return neighbour, (neighbour >= 0) & (neighbour < doms)

    def halo_copy(which, level, side, landing):
        field = fields[which][level]
        return pltpu.make_async_remote_copy(
            src_ref=field.at[pl.ds(HALO + (depth - HALO) * side, HALO)],
            dst_ref=field.at[pl.ds((HALO + depth) * landing, HALO)],
            send_sem=halo_send.at[which, level, side],
            recv_sem=halo_recv.at[which, level, landing],
            device_id=(shot, beside(side)[0]),
            device_id_type=MESH,
        )

    def halo_start(which, level, side):
        @pl.when(beside(side)[1])
        def _():
            halo_copy(which, level, side, 1 - side).start()

    def halo_wait(which, level, side):
        @pl.when(beside(side)[1])
        def _():
            halo_copy(which, level, side, side).wait_recv()

    for which in (0, 1):
        loads[which].wait()
        field = fields[which][LEVELS - 1]
        for start in (0, depth - HALO):
            field[start + HALO : start + 2 * HALO] = given[which][0][
                start : start + HALO
            ].astype(F32)
        if which == 0:
            pl.semaphore_wait(barrier, len(peers))
            for peer in beyond:
                pl.semaphore_signal(known.at[0], inc=1, device_id=peer, device_id_type=MESH)
        for turn in (0, 1):
            halo_start(which, LEVELS - 1, turn ^ core)
    for which in (0, 1):
        fields[which][LEVELS - 1][2 * HALO : depth] = given[which][0][
            HALO : depth - HALO
        ].astype(F32)

    row_side[...] = twice(band(width, (0.0,) + RING), 1)
    column_side[...] = twice(band(span, (0.0,) + RING), 0)
    first = lax.broadcasted_iota(jnp.int32, (width, span), 0) == cell[1]
    second = lax.broadcasted_iota(jnp.int32, (width, span), 1) == cell[2]
    spot[...] = jnp.where(first & second, 1.0, 0.0)
    lines = lax.broadcasted_iota(jnp.int32, (span, receiver.shape[2]), 0)
    for level in range(1, LEVELS):
        spread = jnp.where(lines == receiver[2], residual[level : level + 1, :], 0.0)
        inject_side[level] = columns_of(split(jnp.transpose(spread)))
    lines = lax.broadcasted_iota(jnp.int32, (width, receiver.shape[2]), 0)

    @pl.loop(0, depth)
    def _(z):
        hit = (lines == receiver[1]) & (receiver[0] == anchor + z)
        marks[z] = jnp.where(hit, 1.0, 0.0).astype(BF16)

    place = lax.broadcasted_iota(jnp.int32, (width, width), 0)
    row = place % rows
    y_hi = place // rows % parts_y
    for way, parts in enumerate(first_two):
        minor = place // (rows * parts_y) % parts[1]
        major = place // (rows * parts_y * parts[1])
        x_of, z_of = (major, minor) if way == 0 else (minor, major)
        wanted = ((y_hi * parts_x + x_of) * parts_z + z_of) * rows + row
        distance = jnp.abs(wanted - lax.broadcasted_iota(jnp.int32, (width, width), 1))
        taps = jnp.zeros((width, width), F32)
        for d, weight in enumerate((0.375, 0.25, 0.0625)):
            taps = jnp.where(distance == d, weight, taps)
        blur_row[way] = twice(taps, 1)
    blur_column[...] = twice(band(span, (0.375, 0.25, 0.0625)), 0)
    for way, parts in enumerate(first_two):
        count = HALO * width // parts[0]
        place = lax.broadcasted_iota(jnp.int32, (count, count), 0)
        row = place % rows
        layer = place // rows % HALO
        y_hi = place // (rows * HALO) % parts_y
        minor = place // (rows * HALO * parts_y)
        wanted = ((layer * parts[1] + minor) * parts_y + y_hi) * rows + row
        hit = wanted == lax.broadcasted_iota(jnp.int32, (count, count), 1)
        order[way][...] = twice(jnp.where(hit, 1.0, 0.0), 1)

    def both_sides(blocks, left, right):
        flat = rows_of([columns_of(block) for block in blocks])
        upright = columns_of([rows_of(block) for block in blocks])
        flat, upright = dot(flat, right), dot(left, upright)
        return [
            flat[at * width : (at + 1) * width] + upright[:, at * span : (at + 1) * span]
            for at in range(len(blocks))
        ]

    def advance(which, level, start):
        field = fields[which][level]
        layers = range(HALO)
        if level == LEVELS - 1:
            blocks = [(given[which][0][start + at],) for at in layers]
            lateral = both_sides(blocks, row_side[:, :width], column_side[:span])
        else:
            blocks = [split(field[start + at + HALO]) for at in layers]
            lateral = both_sides(blocks, row_side[...], column_side[...])
        if which == 1:
            inject = dot(rows_of([marks[start + at] for at in layers]), inject_side[level])
            inject = inject[:, :span] + inject[:, span:]
            inject = [inject[at * width : (at + 1) * width] for at in layers]
        else:
            inject = [
                jnp.where(cell[0] == anchor + start + at, wave[level], 0.0) * spot[...]
                for at in layers
            ]
        blurred = []
        for at in layers:
            z = start + at
            current = field[z + HALO]
            summed = lateral[at] + CENTER * current
            for shift in range(1, HALO + 1):
                summed = summed + RING[shift - 1] * (
                    field[z + HALO + shift] + field[z + HALO - shift]
                )
            term = kappa[z] * (summed * (1.0 / SCALE)) + inject[at]
            if which == 0:
                product = fields[1][level][z + HALO] * term
                if level < LEVELS - 1:
                    product = product + totals[level][z]
                if level > 0:
                    totals[level - 1][z] = product
                else:
                    blurred.append(product)
            if level > 0:
                if level == LEVELS - 1:
                    later = given[which][1][z].astype(F32)
                else:
                    later = fields[which][level + 1][z + HALO]
                fields[which][level - 1][z + HALO] = 2.0 * current - later + term
        return blurred

    def blur(blurred, start, way):
        flat = dot(rows_of([columns_of(split(at)) for at in blurred]), blur_column[...])
        blocks = [flat[at * width : (at + 1) * width] for at in range(HALO)]
        upright = dot(blur_row[way], columns_of([rows_of(split(at)) for at in blocks]))
        for at in range(HALO):
            part[start + at] = upright[:, at * span : (at + 1) * span]

    def remote(source, target, send_sem, recv_sem, peer):
        return pltpu.make_async_remote_copy(
            src_ref=source,
            dst_ref=target,
            send_sem=send_sem,
            recv_sem=recv_sem,
            device_id=peer,
            device_id_type=MESH,
        )

    inner, outer = (depth - HALO) * (1 - core), (depth - HALO) * core
    starts = (HALO, 2 * HALO, inner, outer)
    ways = (1, 0, 0, 0)
    spots = (x_at, z_at)

    def first_copy(chunk, step):
        way = ways[chunk]
        stripe = width // first_two[way][0]
        place = (spots[way] + step) % first_two[way][0] * stripe
        return remote(
            part.at[pl.ds(starts[chunk], HALO), pl.ds(pl.multiple_of(place, stripe), stripe)],
            first_in[way].at[max(chunk - 1, 0), step - 1],
            first_send.at[chunk, step - 1],
            first_recv.at[chunk, step - 1],
            (by_x, by_z)[way](step),
        )

    def second_copy(chunk, step):
        way = ways[chunk]
        return remote(
            second_out[way].at[max(chunk - 1, 0), (spots[1 - way] + step) % first_two[way][1]],
            second_in[way].at[max(chunk - 1, 0), step - 1],
            second_send.at[chunk, step - 1],
            second_recv.at[chunk, step - 1],
            (by_z, by_x)[way](step),
        )

    def y_copy(chunk, step):
        return remote(
            y_out.at[chunk],
            y_in.at[chunk, step - 1],
            y_send.at[chunk, step - 1],
            y_recv.at[chunk, step - 1],
            by_y(step),
        )

    def first_steps(chunk):
        return range(1, first_two[ways[chunk]][0])

    def second_steps(chunk):
        return range(1, first_two[ways[chunk]][1])

    def finish(chunk):
        start = starts[chunk]
        blur(advance(0, 0, start), start, ways[chunk])
        for step in first_steps(chunk):
            first_copy(chunk, step).start()

    def inside(which, level):
        @pl.loop(HALO, depth - HALO, step=HALO)
        def _(start):
            advance(which, level, start)

    def sides(which, level):
        @pl.loop(0, 2)
        def _(turn):
            side = turn ^ core
            halo_wait(which, level, side)
            advance(which, level, (depth - HALO) * side)
            if level > 1 or which == 0:
                halo_start(which, level - 1, side)

    for load in loads[2:]:
        load.wait()
    for level in reversed(range(2, LEVELS)):
        for which in (0, 1):
            inside(which, level)
            sides(which, level)
            if level == LEVELS - 1 and which == 0:
                pl.semaphore_wait(known.at[0], len(beyond))
                for peer in farther:
                    pl.semaphore_signal(known.at[1], inc=1, device_id=peer, device_id_type=MESH)
    inside(0, 1)
    inside(1, 1)
    sides(0, 1)
    if farther:
        pl.semaphore_wait(known.at[1], len(farther))
    finish(1)
    finish(0)
    for chunk, side in ((2, 1 - core), (3, core)):
        halo_wait(1, 1, side)
        advance(1, 1, starts[chunk])
        halo_wait(0, 0, side)
        finish(chunk)

    for chunk in (1, 2, 0, 3):
        way = ways[chunk]
        parts = first_two[way]
        stripe = width // parts[0]
        own = pl.multiple_of(spots[way] * stripe, stripe)
        summed = part[pl.ds(starts[chunk], HALO), pl.ds(own, stripe)]
        for step in first_steps(chunk):
            first_copy(chunk, step).wait_recv()
            summed = summed + first_in[way][max(chunk - 1, 0), step - 1]
        moved = dot(order[way][...], rows_of(split(summed.reshape(HALO * stripe, span))))
        second_out[way][max(chunk - 1, 0)] = moved.reshape(parts[1], HALO * stripe // parts[1], span)
        for step in second_steps(chunk):
            second_copy(chunk, step).start()
    block = rows * HALO
    for chunk in (1, 2, 0, 3):
        way = ways[chunk]
        summed = second_out[way][max(chunk - 1, 0), spots[1 - way]]
        for step in second_steps(chunk):
            second_copy(chunk, step).wait_recv()
            summed = summed + second_in[way][max(chunk - 1, 0), step - 1]
        y_out[chunk] = summed.reshape(parts_y, block, span)
        for step in range(1, parts_y):
            y_copy(chunk, step).start()
    power = jnp.zeros((block, span), F32)
    for chunk in (1, 2, 0, 3):
        summed = y_out[chunk]
        for step in range(1, parts_y):
            y_copy(chunk, step).wait_recv()
            summed = summed + y_in[chunk, step - 1]
        y_sum[chunk] = summed
        for y_hi in range(parts_y):
            power = power + summed[y_hi] * summed[y_hi]
    power_copies = []
    for stage, peers in enumerate(stages):
        power_out[stage] = power
        now = [
            remote(
                power_out.at[stage],
                power_in.at[stage, step],
                p_send.at[stage, step],
                p_recv.at[stage, step],
                peer,
            )
            for step, peer in enumerate(peers)
        ]
        for copy in now:
            copy.start()
        for step, copy in enumerate(now):
            copy.wait_recv()
            power = power + power_in[stage, step]
        power_copies += now
    scale = lax.rsqrt(jnp.full((1, 1), jnp.sum(power)) * (1.0 / cells) + 1e-6)
    for chunk, start in enumerate(starts):
        place = start * rows
        if not isinstance(place, int):
            place = pl.multiple_of(place, block)
        out[pl.ds(place, block)] = -y_sum[chunk, y_at] * scale

    for chunk in range(len(starts)):
        for step in first_steps(chunk):
            first_copy(chunk, step).wait_send()
        for step in second_steps(chunk):
            second_copy(chunk, step).wait_send()
        for step in range(1, parts_y):
            y_copy(chunk, step).wait_send()
    for copy in power_copies:
        copy.wait_send()
    for level in reversed(range(LEVELS)):
        for which in (0, 1) if level > 0 else (0,):
            for side in (0, 1):

                @pl.when(beside(side)[1])
                def _():
                    halo_copy(which, level, side, 1 - side).wait_send()


def per_device(doms, kappa, source_pair, adjoint_pair, wavelet, residuals, source_cell, receiver_cells):
    depth, width, span = kappa.shape
    receivers = receiver_cells.shape[2]
    parts_y, parts_x, parts_z = SHOT_PARTS
    rows = width // (parts_y * parts_x * parts_z)
    chunks = depth // HALO
    counts = (HALO * width // parts_x, HALO * width // parts_z)
    block = rows * HALO
    most = max(doms, parts_z, parts_x) - 1
    hbm = pl.BlockSpec(memory_space=pl.ANY)
    vmem = pl.BlockSpec(memory_space=pltpu.VMEM)
    smem = pl.BlockSpec(memory_space=pltpu.SMEM)
    dma = pltpu.SemaphoreType.DMA
    slab = pltpu.VMEM(kappa.shape, F32)
    padded = pltpu.VMEM((depth + 2 * HALO, width, span), F32)
    first = pltpu.VMEM(kappa.shape, BF16)
    direction = pl.pallas_call(
        functools.partial(kernel, doms, float(depth * doms * width * span)),
        out_shape=jax.ShapeDtypeStruct((depth * rows, span), F32),
        in_specs=[hbm, hbm, hbm, smem, vmem, smem, vmem],
        out_specs=vmem,
        scratch_shapes=[
            slab,
            [[first] * 2] * 2,
            [[padded] * LEVELS] * 2,
            [slab] * (LEVELS - 1),
            slab,
            pltpu.VMEM((width, span), F32),
            pltpu.VMEM((depth, width, receivers), BF16),
            pltpu.VMEM((width, 2 * width), BF16),
            pltpu.VMEM((2 * span, span), BF16),
            pltpu.VMEM((LEVELS, receivers, 2 * span), BF16),
            pltpu.VMEM((2, width, 2 * width), BF16),
            pltpu.VMEM((2 * span, span), BF16),
            [pltpu.VMEM((count, 2 * count), BF16) for count in counts],
            [
                pltpu.VMEM((most, parts - 1, HALO, width // parts, span), F32)
                for most, parts in ((chunks - 1, parts_x), (1, parts_z))
            ],
            [
                pltpu.VMEM((most, parts, block * parts_y, span), F32)
                for most, parts in ((chunks - 1, parts_z), (1, parts_x))
            ],
            [
                pltpu.VMEM((most, parts - 1, block * parts_y, span), F32)
                for most, parts in ((chunks - 1, parts_z), (1, parts_x))
            ],
            pltpu.VMEM((chunks, parts_y, block, span), F32),
            pltpu.VMEM((chunks, parts_y - 1, parts_y, block, span), F32),
            pltpu.VMEM((chunks, parts_y, block, span), F32),
            pltpu.VMEM((3, block, span), F32),
            pltpu.VMEM((3, most, block, span), F32),
            dma((5,)),
            pltpu.SemaphoreType.REGULAR((2,)),
            dma((2, LEVELS, 2)),
            dma((2, LEVELS, 2)),
            dma((chunks, most)),
            dma((chunks, most)),
            dma((chunks, most)),
            dma((chunks, most)),
            dma((chunks, parts_y - 1)),
            dma((chunks, parts_y - 1)),
            dma((3, most)),
            dma((3, most)),
        ],
        compiler_params=pltpu.CompilerParams(
            collective_id=0, has_side_effects=True, vmem_limit_bytes=56164352
        ),
    )(
        kappa,
        source_pair[0],
        adjoint_pair[0],
        wavelet[0],
        residuals[0],
        source_cell[0],
        jnp.transpose(receiver_cells, (1, 0, 2)),
    )
    return direction.reshape(depth, rows, span)


def solution(mesh):
    return jax.shard_map(
        functools.partial(per_device, mesh.shape["dom"]),
        mesh=mesh,
        in_specs=(
            P("dom", None, None),
            P("shot", None, "dom", None, None),
            P("shot", None, "dom", None, None),
            P("shot", None),
            P("shot", None, None),
            P("shot", None),
            P("shot", None, None),
        ),
        out_specs=P("dom", "shot", None),
        check_vma=False,
    )
```

```python
import functools

import jax
import jax.numpy as jnp
from jax import lax
from jax.experimental import pallas as pl
from jax.experimental.pallas import tpu as pltpu
from jax.sharding import PartitionSpec as P

MESH = pl.DeviceIdType.MESH
LEVELS = 4
HALO = 4
SCALE = 5040.0
RING = (8064.0, -1008.0, 128.0, -9.0)
CENTER = 3.0 * -14350.0
SHOT_PARTS = (2, 4, 8)
F32 = jnp.float32
BF16 = jnp.bfloat16


def split(value):
    high = value.astype(BF16)
    low = (value - high.astype(F32)).astype(BF16)
    return high, low


def band(size, weights):
    rows = lax.broadcasted_iota(jnp.int32, (size, size), 0)
    columns = lax.broadcasted_iota(jnp.int32, (size, size), 1)
    distance = jnp.abs(rows - columns)
    matrix = jnp.zeros((size, size), F32)
    for d, weight in enumerate(weights):
        matrix = jnp.where(distance == d, weight, matrix)
    return matrix


def twice(matrix, axis):
    matrix = matrix.astype(BF16)
    return jnp.concatenate((matrix, matrix), axis=axis)


def dot(a, b):
    return jnp.dot(a, b, preferred_element_type=F32)


def rows_of(blocks):
    return jnp.concatenate(blocks, axis=0)


def columns_of(blocks):
    return jnp.concatenate(blocks, axis=1)


def kernel(
    doms, cells,
    kappa_hbm, source_hbm, adjoint_hbm, wave_hbm, residual_hbm, cell_hbm, receiver_hbm, out,
    wave, residual, cell, receiver, kappa, given, fields, totals, part, spot, marks, row_side, column_side, inject_side,
    blur_row, blur_column, order,
    first_in, second_out, second_in, y_out, y_in, y_sum, power_out, power_in,
    load_sem, known, halo_send, halo_recv,
    first_send, first_recv, second_send, second_recv, y_send, y_recv, p_send, p_recv,
):
    depth, width, span = kappa.shape
    shot, dom = lax.axis_index("shot"), lax.axis_index("dom")
    core = dom % 2
    anchor = dom * depth
    parts_y, parts_x, parts_z = SHOT_PARTS
    rows = width // (parts_y * parts_x * parts_z)
    z_at, x_at, y_at = shot % parts_z, shot // parts_z % parts_x, shot // (parts_z * parts_x)
    first_two = ((parts_x, parts_z), (parts_z, parts_x))
    ring = parts_y * doms // 2

    def by_x(step):
        return ((y_at * parts_x + (x_at + step) % parts_x) * parts_z + z_at, dom)

    def by_z(step):
        return ((y_at * parts_x + x_at) * parts_z + (z_at + step) % parts_z, dom)

    def by_y(step):
        return (((y_at + step) % parts_y * parts_x + x_at) * parts_z + z_at, dom)

    def by_x_and_dom(step):
        return (by_x(step // doms)[0], (dom + step) % doms)

    def by_ring(step, turn):
        at = (y_at * (doms // 2) + dom // 2 + step) % ring
        y_hi, chip = at // (doms // 2), at % (doms // 2)
        return ((y_hi * parts_x + x_at) * parts_z + z_at, chip * 2 + (core + turn) % 2)

    def near(size):
        return sorted({1, size - 1})

    def next_to(size):
        return [2, size - 2] if size > 4 else []

    loads = []
    for at, (source, target) in enumerate(
        (
            (source_hbm.at[0], given[0][0]),
            (adjoint_hbm.at[0], given[1][0]),
            (receiver_hbm, receiver),
            (residual_hbm, residual),
            (wave_hbm, wave),
            (cell_hbm, cell),
            (kappa_hbm, kappa),
            (source_hbm.at[1], given[0][1]),
            (adjoint_hbm.at[1], given[1][1]),
        )
    ):
        copy = pltpu.make_async_copy(source, target, load_sem.at[at])
        copy.start()
        loads.append(copy)

    barrier = pltpu.get_barrier_semaphore()
    stages = (
        [by_z(step) for step in range(1, parts_z)],
        [by_x_and_dom(step) for step in range(1, parts_x * doms)],
    )
    beyond = [by_ring(step, 0) for step in near(ring)]
    beyond += [by_z(step) for step in near(parts_z)] + [by_x(step) for step in near(parts_x)]
    peers = [by_ring(2 * core - 1, 1), by_ring(0, 1)] + beyond
    farther = [by_ring(step, 0) for step in next_to(ring)]
    farther += [by_z(step) for step in next_to(parts_z)]
    for peer in peers:
        pl.semaphore_signal(barrier, inc=1, device_id=peer, device_id_type=MESH)

    @pl.when(dom == 0)
    def _():
        for which in (0, 1):
            for level in range(LEVELS):
                fields[which][level][0:HALO] = jnp.zeros((HALO, width, span), F32)

    @pl.when(dom == doms - 1)
    def _():
        for which in (0, 1):
            for level in range(LEVELS):
                fields[which][level][HALO + depth :] = jnp.zeros((HALO, width, span), F32)

    def beside(side):
        neighbour = dom + 2 * side - 1
        return neighbour, (neighbour >= 0) & (neighbour < doms)

    def halo_copy(which, level, side, landing):
        field = fields[which][level]
        return pltpu.make_async_remote_copy(
            src_ref=field.at[pl.ds(HALO + (depth - HALO) * side, HALO)],
            dst_ref=field.at[pl.ds((HALO + depth) * landing, HALO)],
            send_sem=halo_send.at[which, level, side],
            recv_sem=halo_recv.at[which, level, landing],
            device_id=(shot, beside(side)[0]),
            device_id_type=MESH,
        )

    def halo_start(which, level, side):
        @pl.when(beside(side)[1])
        def _():
            halo_copy(which, level, side, 1 - side).start()

    def halo_wait(which, level, side):
        @pl.when(beside(side)[1])
        def _():
            halo_copy(which, level, side, side).wait_recv()

    for which in (0, 1):
        loads[which].wait()
        field = fields[which][LEVELS - 1]
        for start in (0, depth - HALO):
            field[start + HALO : start + 2 * HALO] = given[which][0][
                start : start + HALO
            ].astype(F32)
        if which == 0:
            pl.semaphore_wait(barrier, len(peers))
            for peer in beyond:
                pl.semaphore_signal(known.at[0], inc=1, device_id=peer, device_id_type=MESH)
        for turn in (0, 1):
            halo_start(which, LEVELS - 1, turn ^ core)
    for which in (0, 1):
        fields[which][LEVELS - 1][2 * HALO : depth] = given[which][0][
            HALO : depth - HALO
        ].astype(F32)

    for load in loads[2:6]:
        load.wait()
    row_side[...] = twice(band(width, (0.0,) + RING), 1)
    column_side[...] = twice(band(span, (0.0,) + RING), 0)
    first = lax.broadcasted_iota(jnp.int32, (width, span), 0) == cell[1]
    second = lax.broadcasted_iota(jnp.int32, (width, span), 1) == cell[2]
    spot[...] = jnp.where(first & second, 1.0, 0.0)
    lines = lax.broadcasted_iota(jnp.int32, (span, receiver.shape[2]), 0)
    for level in range(1, LEVELS):
        spread = jnp.where(lines == receiver[2], residual[level : level + 1, :], 0.0)
        inject_side[level] = columns_of(split(jnp.transpose(spread)))
    lines = lax.broadcasted_iota(jnp.int32, (width, receiver.shape[2]), 0)

    @pl.loop(0, depth)
    def _(z):
        hit = (lines == receiver[1]) & (receiver[0] == anchor + z)
        marks[z] = jnp.where(hit, 1.0, 0.0).astype(BF16)

    place = lax.broadcasted_iota(jnp.int32, (width, width), 0)
    row = place % rows
    y_hi = place // rows % parts_y
    for way, parts in enumerate(first_two):
        minor = place // (rows * parts_y) % parts[1]
        major = place // (rows * parts_y * parts[1])
        x_of, z_of = (major, minor) if way == 0 else (minor, major)
        wanted = ((y_hi * parts_x + x_of) * parts_z + z_of) * rows + row
        distance = jnp.abs(wanted - lax.broadcasted_iota(jnp.int32, (width, width), 1))
        taps = jnp.zeros((width, width), F32)
        for d, weight in enumerate((0.375, 0.25, 0.0625)):
            taps = jnp.where(distance == d, weight, taps)
        blur_row[way] = twice(taps, 1)
    blur_column[...] = twice(band(span, (0.375, 0.25, 0.0625)), 0)
    for way, parts in enumerate(first_two):
        count = HALO * width // parts[0]
        place = lax.broadcasted_iota(jnp.int32, (count, count), 0)
        row = place % rows
        layer = place // rows % HALO
        y_hi = place // (rows * HALO) % parts_y
        minor = place // (rows * HALO * parts_y)
        wanted = ((layer * parts[1] + minor) * parts_y + y_hi) * rows + row
        hit = wanted == lax.broadcasted_iota(jnp.int32, (count, count), 1)
        order[way][...] = twice(jnp.where(hit, 1.0, 0.0), 1)

    def both_sides(blocks, left, right):
        flat = rows_of([columns_of(block) for block in blocks])
        upright = columns_of([rows_of(block) for block in blocks])
        flat, upright = dot(flat, right), dot(left, upright)
        return [
            flat[at * width : (at + 1) * width] + upright[:, at * span : (at + 1) * span]
            for at in range(len(blocks))
        ]

    def advance(which, level, start):
        field = fields[which][level]
        layers = range(HALO)
        if level == LEVELS - 1:
            blocks = [(given[which][0][start + at],) for at in layers]
            lateral = both_sides(blocks, row_side[:, :width], column_side[:span])
        else:
            blocks = [split(field[start + at + HALO]) for at in layers]
            lateral = both_sides(blocks, row_side[...], column_side[...])
        if which == 1:
            inject = dot(rows_of([marks[start + at] for at in layers]), inject_side[level])
            inject = inject[:, :span] + inject[:, span:]
            inject = [inject[at * width : (at + 1) * width] for at in layers]
        else:
            inject = [
                jnp.where(cell[0] == anchor + start + at, wave[level], 0.0) * spot[...]
                for at in layers
            ]
        blurred = []
        for at in layers:
            z = start + at
            current = field[z + HALO]
            summed = lateral[at] + CENTER * current
            for shift in range(1, HALO + 1):
                summed = summed + RING[shift - 1] * (
                    field[z + HALO + shift] + field[z + HALO - shift]
                )
            term = kappa[z] * (summed * (1.0 / SCALE)) + inject[at]
            if which == 0:
                product = fields[1][level][z + HALO] * term
                if level < LEVELS - 1:
                    product = product + totals[level][z]
                if level > 0:
                    totals[level - 1][z] = product
                else:
                    blurred.append(product)
            if level > 0:
                if level == LEVELS - 1:
                    later = given[which][1][z].astype(F32)
                else:
                    later = fields[which][level + 1][z + HALO]
                fields[which][level - 1][z + HALO] = 2.0 * current - later + term
        return blurred

    def blur(blurred, start, way):
        flat = dot(rows_of([columns_of(split(at)) for at in blurred]), blur_column[...])
        blocks = [flat[at * width : (at + 1) * width] for at in range(HALO)]
        upright = dot(blur_row[way], columns_of([rows_of(split(at)) for at in blocks]))
        for at in range(HALO):
            part[start + at] = upright[:, at * span : (at + 1) * span]

    def remote(source, target, send_sem, recv_sem, peer):
        return pltpu.make_async_remote_copy(
            src_ref=source,
            dst_ref=target,
            send_sem=send_sem,
            recv_sem=recv_sem,
            device_id=peer,
            device_id_type=MESH,
        )

    inner, outer = (depth - HALO) * (1 - core), (depth - HALO) * core
    starts = (HALO, 2 * HALO, inner, outer)
    ways = (1, 0, 0, 0)
    spots = (x_at, z_at)

    def first_copy(chunk, step):
        way = ways[chunk]
        stripe = width // first_two[way][0]
        place = (spots[way] + step) % first_two[way][0] * stripe
        return remote(
            part.at[pl.ds(starts[chunk], HALO), pl.ds(pl.multiple_of(place, stripe), stripe)],
            first_in[way].at[max(chunk - 1, 0), step - 1],
            first_send.at[chunk],
            first_recv.at[chunk],
            (by_x, by_z)[way](step),
        )

    def second_copy(chunk, step):
        way = ways[chunk]
        return remote(
            second_out[way].at[max(chunk - 1, 0), (spots[1 - way] + step) % first_two[way][1]],
            second_in[way].at[max(chunk - 1, 0), step - 1],
            second_send.at[chunk],
            second_recv.at[chunk],
            (by_z, by_x)[way](step),
        )

    def together(into, send_sem, recv_sem):
        return remote(into, into, send_sem, recv_sem, by_x(1))

    def first_all(chunk):
        into = first_in[ways[chunk]].at[max(chunk - 1, 0)]
        return together(into, first_send.at[chunk], first_recv.at[chunk])

    def second_all(chunk):
        into = second_in[ways[chunk]].at[max(chunk - 1, 0)]
        return together(into, second_send.at[chunk], second_recv.at[chunk])

    def y_copy(chunk, step):
        return remote(
            y_out.at[chunk],
            y_in.at[chunk, step - 1],
            y_send.at[chunk, step - 1],
            y_recv.at[chunk, step - 1],
            by_y(step),
        )

    def first_steps(chunk):
        return range(1, first_two[ways[chunk]][0])

    def second_steps(chunk):
        return range(1, first_two[ways[chunk]][1])

    def finish(chunk):
        start = starts[chunk]
        blur(advance(0, 0, start), start, ways[chunk])
        for step in first_steps(chunk):
            first_copy(chunk, step).start()

    def inside(which, level):
        @pl.loop(HALO, depth - HALO, step=HALO)
        def _(start):
            advance(which, level, start)

    def sides(which, level):
        @pl.loop(0, 2)
        def _(turn):
            side = turn ^ core
            halo_wait(which, level, side)
            advance(which, level, (depth - HALO) * side)
            if level > 1 or which == 0:
                halo_start(which, level - 1, side)

    for load in loads[6:]:
        load.wait()
    for level in reversed(range(2, LEVELS)):
        for which in (0, 1):
            inside(which, level)
            sides(which, level)
            if level == LEVELS - 1 and which == 0:
                pl.semaphore_wait(known.at[0], len(beyond))
                for peer in farther:
                    pl.semaphore_signal(known.at[1], inc=1, device_id=peer, device_id_type=MESH)
    inside(0, 1)
    inside(1, 1)
    sides(0, 1)
    if farther:
        pl.semaphore_wait(known.at[1], len(farther))
    finish(1)
    finish(0)
    for chunk, side in ((2, 1 - core), (3, core)):
        halo_wait(1, 1, side)
        advance(1, 1, starts[chunk])
        halo_wait(0, 0, side)
        finish(chunk)

    for level in reversed(range(LEVELS)):
        for which in (0, 1) if level > 0 else (0,):
            for side in (0, 1):

                @pl.when(beside(side)[1])
                def _():
                    halo_copy(which, level, side, 1 - side).wait_send()

    for chunk in (1, 2, 3, 0):
        way = ways[chunk]
        parts = first_two[way]
        stripe = width // parts[0]
        own = pl.multiple_of(spots[way] * stripe, stripe)
        summed = part[pl.ds(starts[chunk], HALO), pl.ds(own, stripe)]
        first_all(chunk).wait_recv()
        for step in first_steps(chunk):
            summed = summed + first_in[way][max(chunk - 1, 0), step - 1]
        moved = dot(order[way][...], rows_of(split(summed.reshape(HALO * stripe, span))))
        second_out[way][max(chunk - 1, 0)] = moved.reshape(parts[1], HALO * stripe // parts[1], span)
        for step in second_steps(chunk):
            second_copy(chunk, step).start()
    for chunk in range(len(starts)):
        first_all(chunk).wait_send()
    block = rows * HALO
    for chunk in (1, 2, 0, 3):
        way = ways[chunk]
        summed = second_out[way][max(chunk - 1, 0), spots[1 - way]]
        second_all(chunk).wait_recv()
        for step in second_steps(chunk):
            summed = summed + second_in[way][max(chunk - 1, 0), step - 1]
        y_out[chunk] = summed.reshape(parts_y, block, span)
        for step in range(1, parts_y):
            y_copy(chunk, step).start()
    power = jnp.zeros((block, span), F32)
    for chunk in (1, 2, 0, 3):
        summed = y_out[chunk]
        for step in range(1, parts_y):
            y_copy(chunk, step).wait_recv()
            summed = summed + y_in[chunk, step - 1]
        y_sum[chunk] = summed
        for y_hi in range(parts_y):
            power = power + summed[y_hi] * summed[y_hi]
    for stage, peers in enumerate(stages):
        power_out[stage] = power
        for step, peer in enumerate(peers):
            remote(
                power_out.at[stage],
                power_in.at[stage, step],
                p_send.at[stage],
                p_recv.at[stage],
                peer,
            ).start()
        if stage == 0:
            for chunk in range(len(starts)):
                second_all(chunk).wait_send()
                for step in range(1, parts_y):
                    y_copy(chunk, step).wait_send()
        else:
            into = power_in.at[0, pl.ds(0, len(stages[0]))]
            together(into, p_send.at[0], p_recv.at[0]).wait_send()
        into = power_in.at[stage, pl.ds(0, len(peers))]
        together(into, p_send.at[stage], p_recv.at[stage]).wait_recv()
        for step in range(len(peers)):
            power = power + power_in[stage, step]
    scale = lax.rsqrt(jnp.full((1, 1), jnp.sum(power)) * (1.0 / cells) + 1e-6)
    for chunk, start in enumerate(starts):
        place = start * rows
        if not isinstance(place, int):
            place = pl.multiple_of(place, block)
        out[pl.ds(place, block)] = -y_sum[chunk, y_at] * scale

    into = power_in.at[1, pl.ds(0, len(stages[1]))]
    together(into, p_send.at[1], p_recv.at[1]).wait_send()


def per_device(doms, kappa, source_pair, adjoint_pair, wavelet, residuals, source_cell, receiver_cells):
    depth, width, span = kappa.shape
    receivers = receiver_cells.shape[2]
    parts_y, parts_x, parts_z = SHOT_PARTS
    rows = width // (parts_y * parts_x * parts_z)
    chunks = depth // HALO
    counts = (HALO * width // parts_x, HALO * width // parts_z)
    block = rows * HALO
    most = max(doms * parts_x, parts_z) - 1
    hbm = pl.BlockSpec(memory_space=pltpu.HBM)
    vmem = pl.BlockSpec(memory_space=pltpu.VMEM)
    dma = pltpu.SemaphoreType.DMA
    slab = pltpu.VMEM(kappa.shape, F32)
    padded = pltpu.VMEM((depth + 2 * HALO, width, span), F32)
    first = pltpu.VMEM(kappa.shape, BF16)
    direction = pl.pallas_call(
        functools.partial(kernel, doms, float(depth * doms * width * span)),
        out_shape=jax.ShapeDtypeStruct((depth * rows, span), F32),
        in_specs=[hbm] * 7,
        out_specs=vmem,
        scratch_shapes=[
            pltpu.SMEM(wavelet.shape[1:], F32),
            pltpu.VMEM(residuals.shape[1:], F32),
            pltpu.SMEM(source_cell.shape[1:], jnp.int32),
            pltpu.VMEM((3, 1, receivers), jnp.int32),
            slab,
            [[first] * 2] * 2,
            [[padded] * LEVELS] * 2,
            [slab] * (LEVELS - 1),
            slab,
            pltpu.VMEM((width, span), F32),
            pltpu.VMEM((depth, width, receivers), BF16),
            pltpu.VMEM((width, 2 * width), BF16),
            pltpu.VMEM((2 * span, span), BF16),
            pltpu.VMEM((LEVELS, receivers, 2 * span), BF16),
            pltpu.VMEM((2, width, 2 * width), BF16),
            pltpu.VMEM((2 * span, span), BF16),
            [pltpu.VMEM((count, 2 * count), BF16) for count in counts],
            [
                pltpu.VMEM((most, parts - 1, HALO, width // parts, span), F32)
                for most, parts in ((chunks - 1, parts_x), (1, parts_z))
            ],
            [
                pltpu.VMEM((most, parts, block * parts_y, span), F32)
                for most, parts in ((chunks - 1, parts_z), (1, parts_x))
            ],
            [
                pltpu.VMEM((most, parts - 1, block * parts_y, span), F32)
                for most, parts in ((chunks - 1, parts_z), (1, parts_x))
            ],
            pltpu.VMEM((chunks, parts_y, block, span), F32),
            pltpu.VMEM((chunks, parts_y - 1, parts_y, block, span), F32),
            pltpu.VMEM((chunks, parts_y, block, span), F32),
            pltpu.VMEM((2, block, span), F32),
            pltpu.VMEM((2, most, block, span), F32),
            dma((9,)),
            pltpu.SemaphoreType.REGULAR((2,)),
            dma((2, LEVELS, 2)),
            dma((2, LEVELS, 2)),
            dma((chunks,)),
            dma((chunks,)),
            dma((chunks,)),
            dma((chunks,)),
            dma((chunks, parts_y - 1)),
            dma((chunks, parts_y - 1)),
            dma((2,)),
            dma((2,)),
        ],
        compiler_params=pltpu.CompilerParams(
            collective_id=0, has_side_effects=True, vmem_limit_bytes=56164352
        ),
    )(
        kappa,
        source_pair[0],
        adjoint_pair[0],
        wavelet[0],
        residuals[0],
        source_cell[0],
        jnp.transpose(receiver_cells, (1, 0, 2)),
    )
    return direction.reshape(depth, rows, span)


def solution(mesh):
    return jax.shard_map(
        functools.partial(per_device, mesh.shape["dom"]),
        mesh=mesh,
        in_specs=(
            P("dom", None, None),
            P("shot", None, "dom", None, None),
            P("shot", None, "dom", None, None),
            P("shot", None),
            P("shot", None, None),
            P("shot", None),
            P("shot", None, None),
        ),
        out_specs=P("dom", "shot", None),
        check_vma=False,
    )
```

```python
import functools

import jax
import jax.numpy as jnp
from jax import lax
from jax.experimental import pallas as pl
from jax.experimental.pallas import tpu as pltpu
from jax.sharding import PartitionSpec as P

MESH = pl.DeviceIdType.MESH
LEVELS = 4
HALO = 4
SCALE = 5040.0
RING = (8064.0, -1008.0, 128.0, -9.0)
CENTER = 3.0 * -14350.0
SHOT_PARTS = (2, 4, 8)
F32 = jnp.float32
BF16 = jnp.bfloat16


def split(value):
    high = value.astype(BF16)
    low = (value - high.astype(F32)).astype(BF16)
    return high, low


def band(size, weights):
    rows = lax.broadcasted_iota(jnp.int32, (size, size), 0)
    columns = lax.broadcasted_iota(jnp.int32, (size, size), 1)
    distance = jnp.abs(rows - columns)
    matrix = jnp.zeros((size, size), F32)
    for d, weight in enumerate(weights):
        matrix = jnp.where(distance == d, weight, matrix)
    return matrix


def twice(matrix, axis):
    matrix = matrix.astype(BF16)
    return jnp.concatenate((matrix, matrix), axis=axis)


def dot(a, b):
    return jnp.dot(a, b, preferred_element_type=F32)


def rows_of(blocks):
    return jnp.concatenate(blocks, axis=0)


def columns_of(blocks):
    return jnp.concatenate(blocks, axis=1)


def kernel(
    doms, cells,
    kappa_hbm, source_hbm, adjoint_hbm, wave_hbm, residual_hbm, cell_hbm, receiver_hbm, out,
    wave, residual, cell, receiver, kappa, given, fields, totals, part, spot, marks, row_side, column_side, inject_side,
    blur_row, blur_column, order,
    first_in, second_out, second_in, y_out, y_in, y_sum, power_out, power_in,
    load_sem, known, halo_send, halo_recv,
    first_send, first_recv, second_send, second_recv, y_send, y_recv, p_send, p_recv,
):
    depth, width, span = kappa.shape
    shot, dom = lax.axis_index("shot"), lax.axis_index("dom")
    core = dom % 2
    anchor = dom * depth
    parts_y, parts_x, parts_z = SHOT_PARTS
    rows = width // (parts_y * parts_x * parts_z)
    z_at, x_at, y_at = shot % parts_z, shot // parts_z % parts_x, shot // (parts_z * parts_x)
    first_two = ((parts_x, parts_z), (parts_z, parts_x))
    ring = parts_y * doms // 2

    def by_x(step):
        return ((y_at * parts_x + (x_at + step) % parts_x) * parts_z + z_at, dom)

    def by_z(step):
        return ((y_at * parts_x + x_at) * parts_z + (z_at + step) % parts_z, dom)

    def by_y(step):
        return (((y_at + step) % parts_y * parts_x + x_at) * parts_z + z_at, dom)

    def by_x_and_dom(step):
        return (by_x(step // doms)[0], (dom + step) % doms)

    def by_ring(step, turn):
        at = (y_at * (doms // 2) + dom // 2 + step) % ring
        y_hi, chip = at // (doms // 2), at % (doms // 2)
        return ((y_hi * parts_x + x_at) * parts_z + z_at, chip * 2 + (core + turn) % 2)

    def near(size):
        return sorted({1, size - 1})

    def next_to(size):
        return [2, size - 2] if size > 4 else []

    loads = []
    for at, (source, target) in enumerate(
        (
            (source_hbm.at[0], given[0][0]),
            (adjoint_hbm.at[0], given[1][0]),
            (receiver_hbm, receiver),
            (residual_hbm, residual),
            (wave_hbm, wave),
            (cell_hbm, cell),
            (kappa_hbm, kappa),
            (source_hbm.at[1], given[0][1]),
            (adjoint_hbm.at[1], given[1][1]),
        )
    ):
        copy = pltpu.make_async_copy(source, target, load_sem.at[at])
        copy.start()
        loads.append(copy)

    barrier = pltpu.get_barrier_semaphore()
    stages = (
        [by_z(step) for step in range(1, parts_z)],
        [by_x_and_dom(step) for step in range(1, parts_x * doms)],
    )
    beyond = [by_ring(step, 0) for step in near(ring)]
    beyond += [by_z(step) for step in near(parts_z)] + [by_x(step) for step in near(parts_x)]
    peers = [by_ring(2 * core - 1, 1), by_ring(0, 1)] + beyond
    farther = [by_ring(step, 0) for step in next_to(ring)]
    farther += [by_z(step) for step in next_to(parts_z)]
    for peer in peers:
        pl.semaphore_signal(barrier, inc=1, device_id=peer, device_id_type=MESH)

    def beside(side):
        neighbour = dom + 2 * side - 1
        return neighbour, (neighbour >= 0) & (neighbour < doms)

    def halo_copy(which, level, side, landing):
        field = fields[which][level]
        return pltpu.make_async_remote_copy(
            src_ref=field.at[pl.ds(HALO + (depth - HALO) * side, HALO)],
            dst_ref=field.at[pl.ds((HALO + depth) * landing, HALO)],
            send_sem=halo_send.at[which, level, side],
            recv_sem=halo_recv.at[which, level, landing],
            device_id=(shot, beside(side)[0]),
            device_id_type=MESH,
        )

    def halo_start(which, level, side):
        @pl.when(beside(side)[1])
        def _():
            halo_copy(which, level, side, 1 - side).start()

    def halo_wait(which, level, side):
        @pl.when(beside(side)[1])
        def _():
            halo_copy(which, level, side, side).wait_recv()

    for which in (0, 1):
        loads[which].wait()
        field = fields[which][LEVELS - 1]
        for start in (0, depth - HALO):
            field[start + HALO : start + 2 * HALO] = given[which][0][
                start : start + HALO
            ].astype(F32)
        if which == 0:
            pl.semaphore_wait(barrier, len(peers))
            for peer in beyond:
                pl.semaphore_signal(known.at[0], inc=1, device_id=peer, device_id_type=MESH)
        for turn in (0, 1):
            halo_start(which, LEVELS - 1, turn ^ core)
    @pl.when(dom == 0)
    def _():
        for which in (0, 1):
            for level in range(LEVELS):
                fields[which][level][0:HALO] = jnp.zeros((HALO, width, span), F32)

    @pl.when(dom == doms - 1)
    def _():
        for which in (0, 1):
            for level in range(LEVELS):
                fields[which][level][HALO + depth :] = jnp.zeros((HALO, width, span), F32)

    for which in (0, 1):
        fields[which][LEVELS - 1][2 * HALO : depth] = given[which][0][
            HALO : depth - HALO
        ].astype(F32)

    for load in loads[2:6]:
        load.wait()
    row_side[...] = twice(band(width, (0.0,) + RING), 1)
    column_side[...] = twice(band(span, (0.0,) + RING), 0)
    first = lax.broadcasted_iota(jnp.int32, (width, span), 0) == cell[1]
    second = lax.broadcasted_iota(jnp.int32, (width, span), 1) == cell[2]
    spot[...] = jnp.where(first & second, 1.0, 0.0)
    lines = lax.broadcasted_iota(jnp.int32, (span, receiver.shape[2]), 0)
    for level in range(1, LEVELS):
        spread = jnp.where(lines == receiver[2], residual[level : level + 1, :], 0.0)
        inject_side[level] = columns_of(split(jnp.transpose(spread)))
    lines = lax.broadcasted_iota(jnp.int32, (width, receiver.shape[2]), 0)

    @pl.loop(0, depth)
    def _(z):
        hit = (lines == receiver[1]) & (receiver[0] == anchor + z)
        marks[z] = jnp.where(hit, 1.0, 0.0).astype(BF16)

    place = lax.broadcasted_iota(jnp.int32, (width, width), 0)
    row = place % rows
    y_hi = place // rows % parts_y
    for way, parts in enumerate(first_two):
        minor = place // (rows * parts_y) % parts[1]
        major = place // (rows * parts_y * parts[1])
        x_of, z_of = (major, minor) if way == 0 else (minor, major)
        wanted = ((y_hi * parts_x + x_of) * parts_z + z_of) * rows + row
        distance = jnp.abs(wanted - lax.broadcasted_iota(jnp.int32, (width, width), 1))
        taps = jnp.zeros((width, width), F32)
        for d, weight in enumerate((0.375, 0.25, 0.0625)):
            taps = jnp.where(distance == d, weight, taps)
        blur_row[way] = twice(taps, 1)
    blur_column[...] = twice(band(span, (0.375, 0.25, 0.0625)), 0)
    for way, parts in enumerate(first_two):
        count = HALO * width // parts[0]
        place = lax.broadcasted_iota(jnp.int32, (count, count), 0)
        row = place % rows
        layer = place // rows % HALO
        y_hi = place // (rows * HALO) % parts_y
        minor = place // (rows * HALO * parts_y)
        wanted = ((layer * parts[1] + minor) * parts_y + y_hi) * rows + row
        hit = wanted == lax.broadcasted_iota(jnp.int32, (count, count), 1)
        order[way][...] = twice(jnp.where(hit, 1.0, 0.0), 1)

    def both_sides(blocks, left, right):
        flat = rows_of([columns_of(block) for block in blocks])
        upright = columns_of([rows_of(block) for block in blocks])
        flat, upright = dot(flat, right), dot(left, upright)
        return [
            flat[at * width : (at + 1) * width] + upright[:, at * span : (at + 1) * span]
            for at in range(len(blocks))
        ]

    def advance(which, level, start):
        field = fields[which][level]
        layers = range(HALO)
        if level == LEVELS - 1:
            blocks = [(given[which][0][start + at],) for at in layers]
            lateral = both_sides(blocks, row_side[:, :width], column_side[:span])
        else:
            blocks = [split(field[start + at + HALO]) for at in layers]
            lateral = both_sides(blocks, row_side[...], column_side[...])
        if which == 1:
            inject = dot(rows_of([marks[start + at] for at in layers]), inject_side[level])
            inject = inject[:, :span] + inject[:, span:]
            inject = [inject[at * width : (at + 1) * width] for at in layers]
        else:
            inject = [
                jnp.where(cell[0] == anchor + start + at, wave[level], 0.0) * spot[...]
                for at in layers
            ]
        blurred = []
        for at in layers:
            z = start + at
            current = field[z + HALO]
            summed = lateral[at] + CENTER * current
            for shift in range(1, HALO + 1):
                summed = summed + RING[shift - 1] * (
                    field[z + HALO + shift] + field[z + HALO - shift]
                )
            term = kappa[z] * (summed * (1.0 / SCALE)) + inject[at]
            if which == 0:
                product = fields[1][level][z + HALO] * term
                if level < LEVELS - 1:
                    product = product + totals[level][z]
                if level > 0:
                    totals[level - 1][z] = product
                else:
                    blurred.append(product)
            if level > 0:
                if level == LEVELS - 1:
                    later = given[which][1][z].astype(F32)
                else:
                    later = fields[which][level + 1][z + HALO]
                fields[which][level - 1][z + HALO] = 2.0 * current - later + term
        return blurred

    def blur(blurred, start, way):
        flat = dot(rows_of([columns_of(split(at)) for at in blurred]), blur_column[...])
        blocks = [flat[at * width : (at + 1) * width] for at in range(HALO)]
        upright = dot(blur_row[way], columns_of([rows_of(split(at)) for at in blocks]))
        for at in range(HALO):
            part[start + at] = upright[:, at * span : (at + 1) * span]

    def remote(source, target, send_sem, recv_sem, peer):
        return pltpu.make_async_remote_copy(
            src_ref=source,
            dst_ref=target,
            send_sem=send_sem,
            recv_sem=recv_sem,
            device_id=peer,
            device_id_type=MESH,
        )

    inner, outer = (depth - HALO) * (1 - core), (depth - HALO) * core
    starts = (HALO, 2 * HALO, inner, outer)
    ways = (1, 0, 0, 0)
    spots = (x_at, z_at)

    def first_copy(chunk, step):
        way = ways[chunk]
        stripe = width // first_two[way][0]
        place = (spots[way] + step) % first_two[way][0] * stripe
        return remote(
            part.at[pl.ds(starts[chunk], HALO), pl.ds(pl.multiple_of(place, stripe), stripe)],
            first_in[way].at[max(chunk - 1, 0), step - 1],
            first_send.at[chunk],
            first_recv.at[chunk],
            (by_x, by_z)[way](step),
        )

    def second_copy(chunk, step):
        way = ways[chunk]
        return remote(
            second_out[way].at[max(chunk - 1, 0), (spots[1 - way] + step) % first_two[way][1]],
            second_in[way].at[max(chunk - 1, 0), step - 1],
            second_send.at[chunk],
            second_recv.at[chunk],
            (by_z, by_x)[way](step),
        )

    def together(into, send_sem, recv_sem):
        return remote(into, into, send_sem, recv_sem, by_x(1))

    def first_all(chunk):
        into = first_in[ways[chunk]].at[max(chunk - 1, 0)]
        return together(into, first_send.at[chunk], first_recv.at[chunk])

    def second_all(chunk):
        into = second_in[ways[chunk]].at[max(chunk - 1, 0)]
        return together(into, second_send.at[chunk], second_recv.at[chunk])

    def y_copy(chunk, step):
        return remote(
            y_out.at[chunk],
            y_in.at[chunk, step - 1],
            y_send.at[chunk, step - 1],
            y_recv.at[chunk, step - 1],
            by_y(step),
        )

    def first_steps(chunk):
        return range(1, first_two[ways[chunk]][0])

    def second_steps(chunk):
        return range(1, first_two[ways[chunk]][1])

    def finish(chunk):
        start = starts[chunk]
        blur(advance(0, 0, start), start, ways[chunk])
        for step in first_steps(chunk):
            first_copy(chunk, step).start()

    def inside(which, level):
        @pl.loop(HALO, depth - HALO, step=HALO)
        def _(start):
            advance(which, level, start)

    def sides(which, level):
        @pl.loop(0, 2)
        def _(turn):
            side = turn ^ core
            halo_wait(which, level, side)
            advance(which, level, (depth - HALO) * side)
            if level > 1 or which == 0:
                halo_start(which, level - 1, side)

    for load in loads[6:]:
        load.wait()
    for level in reversed(range(2, LEVELS)):
        for which in (0, 1):
            inside(which, level)
            sides(which, level)
            if level == LEVELS - 1 and which == 0:
                pl.semaphore_wait(known.at[0], len(beyond))
                for peer in farther:
                    pl.semaphore_signal(known.at[1], inc=1, device_id=peer, device_id_type=MESH)
    inside(0, 1)
    advance(1, 1, starts[1])
    sides(0, 1)
    if farther:
        pl.semaphore_wait(known.at[1], len(farther))
    finish(1)
    advance(1, 1, starts[0])
    finish(0)
    for chunk, side in ((2, 1 - core), (3, core)):
        halo_wait(1, 1, side)
        advance(1, 1, starts[chunk])
        halo_wait(0, 0, side)
        finish(chunk)

    for level in reversed(range(LEVELS)):
        for which in (0, 1) if level > 0 else (0,):
            for side in (0, 1):

                @pl.when(beside(side)[1])
                def _():
                    halo_copy(which, level, side, 1 - side).wait_send()

    for chunk in (1, 2, 3, 0):
        way = ways[chunk]
        parts = first_two[way]
        stripe = width // parts[0]
        own = pl.multiple_of(spots[way] * stripe, stripe)
        summed = part[pl.ds(starts[chunk], HALO), pl.ds(own, stripe)]
        first_all(chunk).wait_recv()
        for step in first_steps(chunk):
            summed = summed + first_in[way][max(chunk - 1, 0), step - 1]
        moved = dot(order[way][...], rows_of(split(summed.reshape(HALO * stripe, span))))
        second_out[way][max(chunk - 1, 0)] = moved.reshape(parts[1], HALO * stripe // parts[1], span)
        for step in second_steps(chunk):
            second_copy(chunk, step).start()
    for chunk in range(len(starts)):
        first_all(chunk).wait_send()
    block = rows * HALO
    for chunk in (1, 2, 0, 3):
        way = ways[chunk]
        summed = second_out[way][max(chunk - 1, 0), spots[1 - way]]
        second_all(chunk).wait_recv()
        for step in second_steps(chunk):
            summed = summed + second_in[way][max(chunk - 1, 0), step - 1]
        y_out[chunk] = summed.reshape(parts_y, block, span)
        for step in range(1, parts_y):
            y_copy(chunk, step).start()
    power = jnp.zeros((block, span), F32)
    for chunk in (1, 2, 0, 3):
        summed = y_out[chunk]
        for step in range(1, parts_y):
            y_copy(chunk, step).wait_recv()
            summed = summed + y_in[chunk, step - 1]
        y_sum[chunk] = summed
        for y_hi in range(parts_y):
            power = power + summed[y_hi] * summed[y_hi]
    power = jnp.sum(power, axis=0, keepdims=True)
    for stage, peers in enumerate(stages):
        power_out[stage] = power
        for step, peer in enumerate(peers):
            remote(
                power_out.at[stage],
                power_in.at[stage, step],
                p_send.at[stage],
                p_recv.at[stage],
                peer,
            ).start()
        if stage == 0:
            for chunk in range(len(starts)):
                second_all(chunk).wait_send()
                for step in range(1, parts_y):
                    y_copy(chunk, step).wait_send()
        else:
            into = power_in.at[0, pl.ds(0, len(stages[0]))]
            together(into, p_send.at[0], p_recv.at[0]).wait_send()
        into = power_in.at[stage, pl.ds(0, len(peers))]
        together(into, p_send.at[stage], p_recv.at[stage]).wait_recv()
        for step in range(len(peers)):
            power = power + power_in[stage, step]
    scale = lax.rsqrt(jnp.full((1, 1), jnp.sum(power)) * (1.0 / cells) + 1e-6)
    for chunk, start in enumerate(starts):
        place = start * rows
        if not isinstance(place, int):
            place = pl.multiple_of(place, block)
        out[pl.ds(place, block)] = -y_sum[chunk, y_at] * scale

    into = power_in.at[1, pl.ds(0, len(stages[1]))]
    together(into, p_send.at[1], p_recv.at[1]).wait_send()


def per_device(doms, kappa, source_pair, adjoint_pair, wavelet, residuals, source_cell, receiver_cells):
    depth, width, span = kappa.shape
    receivers = receiver_cells.shape[2]
    parts_y, parts_x, parts_z = SHOT_PARTS
    rows = width // (parts_y * parts_x * parts_z)
    chunks = depth // HALO
    counts = (HALO * width // parts_x, HALO * width // parts_z)
    block = rows * HALO
    most = max(doms * parts_x, parts_z) - 1
    hbm = pl.BlockSpec(memory_space=pltpu.HBM)
    vmem = pl.BlockSpec(memory_space=pltpu.VMEM)
    dma = pltpu.SemaphoreType.DMA
    slab = pltpu.VMEM(kappa.shape, F32)
    padded = pltpu.VMEM((depth + 2 * HALO, width, span), F32)
    first = pltpu.VMEM(kappa.shape, BF16)
    direction = pl.pallas_call(
        functools.partial(kernel, doms, float(depth * doms * width * span)),
        out_shape=jax.ShapeDtypeStruct((depth * rows, span), F32),
        in_specs=[hbm] * 7,
        out_specs=vmem,
        scratch_shapes=[
            pltpu.SMEM(wavelet.shape[1:], F32),
            pltpu.VMEM(residuals.shape[1:], F32),
            pltpu.SMEM(source_cell.shape[1:], jnp.int32),
            pltpu.VMEM((3, 1, receivers), jnp.int32),
            slab,
            [[first] * 2] * 2,
            [[padded] * LEVELS] * 2,
            [slab] * (LEVELS - 1),
            slab,
            pltpu.VMEM((width, span), F32),
            pltpu.VMEM((depth, width, receivers), BF16),
            pltpu.VMEM((width, 2 * width), BF16),
            pltpu.VMEM((2 * span, span), BF16),
            pltpu.VMEM((LEVELS, receivers, 2 * span), BF16),
            pltpu.VMEM((2, width, 2 * width), BF16),
            pltpu.VMEM((2 * span, span), BF16),
            [pltpu.VMEM((count, 2 * count), BF16) for count in counts],
            [
                pltpu.VMEM((most, parts - 1, HALO, width // parts, span), F32)
                for most, parts in ((chunks - 1, parts_x), (1, parts_z))
            ],
            [
                pltpu.VMEM((most, parts, block * parts_y, span), F32)
                for most, parts in ((chunks - 1, parts_z), (1, parts_x))
            ],
            [
                pltpu.VMEM((most, parts - 1, block * parts_y, span), F32)
                for most, parts in ((chunks - 1, parts_z), (1, parts_x))
            ],
            pltpu.VMEM((chunks, parts_y, block, span), F32),
            pltpu.VMEM((chunks, parts_y - 1, parts_y, block, span), F32),
            pltpu.VMEM((chunks, parts_y, block, span), F32),
            pltpu.VMEM((2, 1, span), F32),
            pltpu.VMEM((2, most, 1, span), F32),
            dma((9,)),
            pltpu.SemaphoreType.REGULAR((2,)),
            dma((2, LEVELS, 2)),
            dma((2, LEVELS, 2)),
            dma((chunks,)),
            dma((chunks,)),
            dma((chunks,)),
            dma((chunks,)),
            dma((chunks, parts_y - 1)),
            dma((chunks, parts_y - 1)),
            dma((2,)),
            dma((2,)),
        ],
        compiler_params=pltpu.CompilerParams(
            collective_id=0, has_side_effects=True, vmem_limit_bytes=56164352
        ),
    )(
        kappa,
        source_pair[0],
        adjoint_pair[0],
        wavelet[0],
        residuals[0],
        source_cell[0],
        jnp.transpose(receiver_cells, (1, 0, 2)),
    )
    return direction.reshape(depth, rows, span)


def solution(mesh):
    return jax.shard_map(
        functools.partial(per_device, mesh.shape["dom"]),
        mesh=mesh,
        in_specs=(
            P("dom", None, None),
            P("shot", None, "dom", None, None),
            P("shot", None, "dom", None, None),
            P("shot", None),
            P("shot", None, None),
            P("shot", None),
            P("shot", None, None),
        ),
        out_specs=P("dom", "shot", None),
        check_vma=False,
    )
```

```python
import functools

import jax
import jax.numpy as jnp
from jax import lax
from jax.experimental import pallas as pl
from jax.experimental.pallas import tpu as pltpu
from jax.sharding import PartitionSpec as P

MESH = pl.DeviceIdType.MESH
LEVELS = 4
HALO = 4
SCALE = 5040.0 / 128.0
RING = (63.0, -7.875, 1.0, -0.0703125)
CENTER = (-336.0, -0.328125)
SHOT_PARTS = (2, 4, 8)
F32 = jnp.float32
BF16 = jnp.bfloat16


def split(value):
    high = value.astype(BF16)
    low = (value - high.astype(F32)).astype(BF16)
    return high, low


def band(size, weights):
    rows = lax.broadcasted_iota(jnp.int32, (size, size), 0)
    columns = lax.broadcasted_iota(jnp.int32, (size, size), 1)
    distance = jnp.abs(rows - columns)
    matrix = jnp.zeros((size, size), F32)
    for d, weight in enumerate(weights):
        matrix = jnp.where(distance == d, weight, matrix)
    return matrix


def twice(matrix, axis):
    matrix = matrix.astype(BF16)
    return jnp.concatenate((matrix, matrix), axis=axis)


def dot(a, b):
    return jnp.dot(a, b, preferred_element_type=F32)


def rows_of(blocks):
    return jnp.concatenate(blocks, axis=0)


def columns_of(blocks):
    return jnp.concatenate(blocks, axis=1)


def kernel(
    doms, cells,
    kappa_hbm, source_hbm, adjoint_hbm, wave_hbm, residual_hbm, cell_hbm, receiver_hbm, out,
    wave, residual, cell, receiver, kappa, given, fields, totals, part, spot, marks, row_side, column_side, inject_side,
    blur_row, blur_column, order,
    first_in, second_out, second_in, y_out, y_in, y_sum, power_out, power_in,
    load_sem, known, halo_send, halo_recv,
    first_send, first_recv, second_send, second_recv, y_send, y_recv, p_send, p_recv,
):
    depth, width, span = kappa.shape
    shot, dom = lax.axis_index("shot"), lax.axis_index("dom")
    core = dom % 2
    anchor = dom * depth
    parts_y, parts_x, parts_z = SHOT_PARTS
    rows = width // (parts_y * parts_x * parts_z)
    z_at, x_at, y_at = shot % parts_z, shot // parts_z % parts_x, shot // (parts_z * parts_x)
    first_two = ((parts_x, parts_z), (parts_z, parts_x))
    ring = parts_y * doms // 2

    def by_x(step):
        return ((y_at * parts_x + (x_at + step) % parts_x) * parts_z + z_at, dom)

    def by_z(step):
        return ((y_at * parts_x + x_at) * parts_z + (z_at + step) % parts_z, dom)

    def by_y(step):
        return (((y_at + step) % parts_y * parts_x + x_at) * parts_z + z_at, dom)

    def by_x_and_dom(step):
        return (by_x(step // doms)[0], (dom + step) % doms)

    def by_ring(step, turn):
        at = (y_at * (doms // 2) + dom // 2 + step) % ring
        y_hi, chip = at // (doms // 2), at % (doms // 2)
        return ((y_hi * parts_x + x_at) * parts_z + z_at, chip * 2 + (core + turn) % 2)

    def near(size):
        return sorted({1, size - 1})

    def next_to(size):
        return [2, size - 2] if size > 4 else []

    loads = []
    for at, (source, target) in enumerate(
        (
            (source_hbm.at[0], given[0][0]),
            (adjoint_hbm.at[0], given[1][0]),
            (receiver_hbm, receiver),
            (residual_hbm, residual),
            (wave_hbm, wave),
            (cell_hbm, cell),
            (kappa_hbm, kappa),
            (source_hbm.at[1], given[0][1]),
            (adjoint_hbm.at[1], given[1][1]),
        )
    ):
        copy = pltpu.make_async_copy(source, target, load_sem.at[at])
        copy.start()
        loads.append(copy)

    barrier = pltpu.get_barrier_semaphore()
    stages = (
        [by_z(step) for step in range(1, parts_z)],
        [by_x_and_dom(step) for step in range(1, parts_x * doms)],
    )
    beyond = [by_ring(step, 0) for step in near(ring)]
    beyond += [by_z(step) for step in near(parts_z)] + [by_x(step) for step in near(parts_x)]
    peers = [by_ring(2 * core - 1, 1), by_ring(0, 1)] + beyond
    farther = [by_ring(step, 0) for step in next_to(ring)]
    farther += [by_z(step) for step in next_to(parts_z)]
    for peer in peers:
        pl.semaphore_signal(barrier, inc=1, device_id=peer, device_id_type=MESH)

    def beside(side):
        neighbour = dom + 2 * side - 1
        return neighbour, (neighbour >= 0) & (neighbour < doms)

    def halo_copy(which, level, side, landing):
        field = fields[which][level]
        return pltpu.make_async_remote_copy(
            src_ref=field.at[pl.ds(HALO + (depth - HALO) * side, HALO)],
            dst_ref=field.at[pl.ds((HALO + depth) * landing, HALO)],
            send_sem=halo_send.at[which, level, side],
            recv_sem=halo_recv.at[which, level, landing],
            device_id=(shot, beside(side)[0]),
            device_id_type=MESH,
        )

    def halo_start(which, level, side):
        @pl.when(beside(side)[1])
        def _():
            halo_copy(which, level, side, 1 - side).start()

    def halo_wait(which, level, side):
        @pl.when(beside(side)[1])
        def _():
            halo_copy(which, level, side, side).wait_recv()

    for which in (0, 1):
        loads[which].wait()
        field = fields[which][LEVELS - 1]
        for start in (0, depth - HALO):
            field[start + HALO : start + 2 * HALO] = given[which][0][
                start : start + HALO
            ].astype(F32)
        if which == 0:
            pl.semaphore_wait(barrier, len(peers))
            for peer in beyond:
                pl.semaphore_signal(known.at[0], inc=1, device_id=peer, device_id_type=MESH)
        for turn in (0, 1):
            halo_start(which, LEVELS - 1, turn ^ core)
    @pl.when(dom == 0)
    def _():
        for which in (0, 1):
            for level in range(LEVELS):
                fields[which][level][0:HALO] = jnp.zeros((HALO, width, span), F32)

    @pl.when(dom == doms - 1)
    def _():
        for which in (0, 1):
            for level in range(LEVELS):
                fields[which][level][HALO + depth :] = jnp.zeros((HALO, width, span), F32)

    for which in (0, 1):
        fields[which][LEVELS - 1][2 * HALO : depth] = given[which][0][
            HALO : depth - HALO
        ].astype(F32)

    for load in loads[2:6]:
        load.wait()
    row_side[...] = twice(band(width, CENTER[1:] + RING), 1)
    column_side[...] = twice(band(span, CENTER[:1] + RING), 0)
    first = lax.broadcasted_iota(jnp.int32, (width, span), 0) == cell[1]
    second = lax.broadcasted_iota(jnp.int32, (width, span), 1) == cell[2]
    spot[...] = jnp.where(first & second, 1.0, 0.0)
    lines = lax.broadcasted_iota(jnp.int32, (span, receiver.shape[2]), 0)
    for level in range(1, LEVELS):
        spread = jnp.where(lines == receiver[2], residual[level : level + 1, :], 0.0)
        inject_side[level] = columns_of(split(jnp.transpose(spread)))
    lines = lax.broadcasted_iota(jnp.int32, (width, receiver.shape[2]), 0)

    @pl.loop(0, depth)
    def _(z):
        hit = (lines == receiver[1]) & (receiver[0] == anchor + z)
        marks[z] = jnp.where(hit, 1.0, 0.0).astype(BF16)

    place = lax.broadcasted_iota(jnp.int32, (width, width), 0)
    row = place % rows
    y_hi = place // rows % parts_y
    for way, parts in enumerate(first_two):
        minor = place // (rows * parts_y) % parts[1]
        major = place // (rows * parts_y * parts[1])
        x_of, z_of = (major, minor) if way == 0 else (minor, major)
        wanted = ((y_hi * parts_x + x_of) * parts_z + z_of) * rows + row
        distance = jnp.abs(wanted - lax.broadcasted_iota(jnp.int32, (width, width), 1))
        taps = jnp.zeros((width, width), F32)
        for d, weight in enumerate((0.375, 0.25, 0.0625)):
            taps = jnp.where(distance == d, weight, taps)
        blur_row[way] = twice(taps, 1)
    blur_column[...] = twice(band(span, (0.375, 0.25, 0.0625)), 0)
    for way, parts in enumerate(first_two):
        count = HALO * width // parts[0]
        place = lax.broadcasted_iota(jnp.int32, (count, count), 0)
        row = place % rows
        layer = place // rows % HALO
        y_hi = place // (rows * HALO) % parts_y
        minor = place // (rows * HALO * parts_y)
        wanted = ((layer * parts[1] + minor) * parts_y + y_hi) * rows + row
        hit = wanted == lax.broadcasted_iota(jnp.int32, (count, count), 1)
        order[way][...] = twice(jnp.where(hit, 1.0, 0.0), 1)

    def both_sides(blocks, left, right):
        flat = rows_of([columns_of(block) for block in blocks])
        upright = columns_of([rows_of(block) for block in blocks])
        flat, upright = dot(flat, right), dot(left, upright)
        return [
            flat[at * width : (at + 1) * width] + upright[:, at * span : (at + 1) * span]
            for at in range(len(blocks))
        ]

    def advance(which, level, start):
        field = fields[which][level]
        layers = range(HALO)
        if level == LEVELS - 1:
            blocks = [(given[which][0][start + at],) for at in layers]
            lateral = both_sides(blocks, row_side[:, :width], column_side[:span])
        else:
            blocks = [split(field[start + at + HALO]) for at in layers]
            lateral = both_sides(blocks, row_side[...], column_side[...])
        if which == 1:
            inject = dot(rows_of([marks[start + at] for at in layers]), inject_side[level])
            inject = inject[:, :span] + inject[:, span:]
            inject = [inject[at * width : (at + 1) * width] for at in layers]
        else:
            inject = [
                jnp.where(cell[0] == anchor + start + at, wave[level], 0.0) * spot[...]
                for at in layers
            ]
        blurred = []
        for at in layers:
            z = start + at
            current = field[z + HALO]
            summed = lateral[at]
            for shift in range(1, HALO + 1):
                pair = field[z + HALO + shift] + field[z + HALO - shift]
                if RING[shift - 1] != 1.0:
                    pair = RING[shift - 1] * pair
                summed = summed + pair
            term = kappa[z] * summed + inject[at]
            if which == 0:
                product = fields[1][level][z + HALO] * term
                if level < LEVELS - 1:
                    product = product + totals[level][z]
                if level > 0:
                    totals[level - 1][z] = product
                else:
                    blurred.append(product)
            if level > 0:
                if level == LEVELS - 1:
                    later = given[which][1][z].astype(F32)
                else:
                    later = fields[which][level + 1][z + HALO]
                fields[which][level - 1][z + HALO] = 2.0 * current - later + term
        return blurred

    def blur(blurred, start, way):
        flat = dot(rows_of([columns_of(split(at)) for at in blurred]), blur_column[...])
        blocks = [flat[at * width : (at + 1) * width] for at in range(HALO)]
        upright = dot(blur_row[way], columns_of([rows_of(split(at)) for at in blocks]))
        for at in range(HALO):
            part[start + at] = upright[:, at * span : (at + 1) * span]

    def remote(source, target, send_sem, recv_sem, peer):
        return pltpu.make_async_remote_copy(
            src_ref=source,
            dst_ref=target,
            send_sem=send_sem,
            recv_sem=recv_sem,
            device_id=peer,
            device_id_type=MESH,
        )

    inner, outer = (depth - HALO) * (1 - core), (depth - HALO) * core
    starts = (HALO, 2 * HALO, inner, outer)
    ways = (1, 0, 0, 0)
    spots = (x_at, z_at)

    def first_copy(chunk, step):
        way = ways[chunk]
        stripe = width // first_two[way][0]
        place = (spots[way] + step) % first_two[way][0] * stripe
        return remote(
            part.at[pl.ds(starts[chunk], HALO), pl.ds(pl.multiple_of(place, stripe), stripe)],
            first_in[way].at[max(chunk - 1, 0), step - 1],
            first_send.at[chunk],
            first_recv.at[chunk],
            (by_x, by_z)[way](step),
        )

    def second_copy(chunk, step):
        way = ways[chunk]
        return remote(
            second_out[way].at[max(chunk - 1, 0), (spots[1 - way] + step) % first_two[way][1]],
            second_in[way].at[max(chunk - 1, 0), step - 1],
            second_send.at[chunk],
            second_recv.at[chunk],
            (by_z, by_x)[way](step),
        )

    def together(into, send_sem, recv_sem):
        return remote(into, into, send_sem, recv_sem, by_x(1))

    def first_all(chunk):
        into = first_in[ways[chunk]].at[max(chunk - 1, 0)]
        return together(into, first_send.at[chunk], first_recv.at[chunk])

    def second_all(chunk):
        into = second_in[ways[chunk]].at[max(chunk - 1, 0)]
        return together(into, second_send.at[chunk], second_recv.at[chunk])

    def y_copy(chunk, step):
        return remote(
            y_out.at[chunk],
            y_in.at[chunk, step - 1],
            y_send.at[chunk, step - 1],
            y_recv.at[chunk, step - 1],
            by_y(step),
        )

    def first_steps(chunk):
        return range(1, first_two[ways[chunk]][0])

    def second_steps(chunk):
        return range(1, first_two[ways[chunk]][1])

    def finish(chunk):
        start = starts[chunk]
        blur(advance(0, 0, start), start, ways[chunk])
        for step in first_steps(chunk):
            first_copy(chunk, step).start()

    def inside(which, level):
        @pl.loop(HALO, depth - HALO, step=HALO)
        def _(start):
            advance(which, level, start)

    def sides(which, level):
        @pl.loop(0, 2)
        def _(turn):
            side = turn ^ core
            halo_wait(which, level, side)
            advance(which, level, (depth - HALO) * side)
            if level > 1 or which == 0:
                halo_start(which, level - 1, side)

    for load in loads[6:]:
        load.wait()
    kappa[...] = kappa[...] * (1.0 / SCALE)
    for level in reversed(range(2, LEVELS)):
        for which in (0, 1):
            inside(which, level)
            sides(which, level)
            if level == LEVELS - 1 and which == 0:
                pl.semaphore_wait(known.at[0], len(beyond))
                for peer in farther:
                    pl.semaphore_signal(known.at[1], inc=1, device_id=peer, device_id_type=MESH)
    inside(0, 1)
    advance(1, 1, starts[1])
    sides(0, 1)
    if farther:
        pl.semaphore_wait(known.at[1], len(farther))
    finish(1)
    advance(1, 1, starts[0])
    finish(0)
    for chunk, side in ((2, 1 - core), (3, core)):
        halo_wait(1, 1, side)
        advance(1, 1, starts[chunk])
        halo_wait(0, 0, side)
        finish(chunk)

    for level in reversed(range(LEVELS)):
        for which in (0, 1) if level > 0 else (0,):
            for side in (0, 1):

                @pl.when(beside(side)[1])
                def _():
                    halo_copy(which, level, side, 1 - side).wait_send()

    for chunk in (1, 2, 3, 0):
        way = ways[chunk]
        parts = first_two[way]
        stripe = width // parts[0]
        own = pl.multiple_of(spots[way] * stripe, stripe)
        summed = part[pl.ds(starts[chunk], HALO), pl.ds(own, stripe)]
        first_all(chunk).wait_recv()
        for step in first_steps(chunk):
            summed = summed + first_in[way][max(chunk - 1, 0), step - 1]
        moved = dot(order[way][...], rows_of(split(summed.reshape(HALO * stripe, span))))
        second_out[way][max(chunk - 1, 0)] = moved.reshape(parts[1], HALO * stripe // parts[1], span)
        for step in second_steps(chunk):
            second_copy(chunk, step).start()
    for chunk in range(len(starts)):
        first_all(chunk).wait_send()
    block = rows * HALO
    for chunk in (1, 2, 0, 3):
        way = ways[chunk]
        summed = second_out[way][max(chunk - 1, 0), spots[1 - way]]
        second_all(chunk).wait_recv()
        for step in second_steps(chunk):
            summed = summed + second_in[way][max(chunk - 1, 0), step - 1]
        y_out[chunk] = summed.reshape(parts_y, block, span)
        for step in range(1, parts_y):
            y_copy(chunk, step).start()
    power = jnp.zeros((block, span), F32)
    for chunk in (1, 2, 0, 3):
        summed = y_out[chunk]
        for step in range(1, parts_y):
            y_copy(chunk, step).wait_recv()
            summed = summed + y_in[chunk, step - 1]
        y_sum[chunk] = summed
        for y_hi in range(parts_y):
            power = power + summed[y_hi] * summed[y_hi]
    power = jnp.sum(power, axis=0, keepdims=True)
    for stage, peers in enumerate(stages):
        power_out[stage] = power
        for step, peer in enumerate(peers):
            remote(
                power_out.at[stage],
                power_in.at[stage, step],
                p_send.at[stage],
                p_recv.at[stage],
                peer,
            ).start()
        if stage == 0:
            for chunk in range(len(starts)):
                second_all(chunk).wait_send()
                for step in range(1, parts_y):
                    y_copy(chunk, step).wait_send()
        else:
            into = power_in.at[0, pl.ds(0, len(stages[0]))]
            together(into, p_send.at[0], p_recv.at[0]).wait_send()
        into = power_in.at[stage, pl.ds(0, len(peers))]
        together(into, p_send.at[stage], p_recv.at[stage]).wait_recv()
        for step in range(len(peers)):
            power = power + power_in[stage, step]
    scale = lax.rsqrt(jnp.full((1, 1), jnp.sum(power)) * (1.0 / cells) + 1e-6)
    for chunk, start in enumerate(starts):
        place = start * rows
        if not isinstance(place, int):
            place = pl.multiple_of(place, block)
        out[pl.ds(place, block)] = -y_sum[chunk, y_at] * scale

    into = power_in.at[1, pl.ds(0, len(stages[1]))]
    together(into, p_send.at[1], p_recv.at[1]).wait_send()


def per_device(doms, kappa, source_pair, adjoint_pair, wavelet, residuals, source_cell, receiver_cells):
    depth, width, span = kappa.shape
    receivers = receiver_cells.shape[2]
    parts_y, parts_x, parts_z = SHOT_PARTS
    rows = width // (parts_y * parts_x * parts_z)
    chunks = depth // HALO
    counts = (HALO * width // parts_x, HALO * width // parts_z)
    block = rows * HALO
    most = max(doms * parts_x, parts_z) - 1
    hbm = pl.BlockSpec(memory_space=pltpu.HBM)
    vmem = pl.BlockSpec(memory_space=pltpu.VMEM)
    dma = pltpu.SemaphoreType.DMA
    slab = pltpu.VMEM(kappa.shape, F32)
    padded = pltpu.VMEM((depth + 2 * HALO, width, span), F32)
    first = pltpu.VMEM(kappa.shape, BF16)
    direction = pl.pallas_call(
        functools.partial(kernel, doms, float(depth * doms * width * span)),
        out_shape=jax.ShapeDtypeStruct((depth * rows, span), F32),
        in_specs=[hbm] * 7,
        out_specs=vmem,
        scratch_shapes=[
            pltpu.SMEM(wavelet.shape[1:], F32),
            pltpu.VMEM(residuals.shape[1:], F32),
            pltpu.SMEM(source_cell.shape[1:], jnp.int32),
            pltpu.VMEM((3, 1, receivers), jnp.int32),
            slab,
            [[first] * 2] * 2,
            [[padded] * LEVELS] * 2,
            [slab] * (LEVELS - 1),
            slab,
            pltpu.VMEM((width, span), F32),
            pltpu.VMEM((depth, width, receivers), BF16),
            pltpu.VMEM((width, 2 * width), BF16),
            pltpu.VMEM((2 * span, span), BF16),
            pltpu.VMEM((LEVELS, receivers, 2 * span), BF16),
            pltpu.VMEM((2, width, 2 * width), BF16),
            pltpu.VMEM((2 * span, span), BF16),
            [pltpu.VMEM((count, 2 * count), BF16) for count in counts],
            [
                pltpu.VMEM((most, parts - 1, HALO, width // parts, span), F32)
                for most, parts in ((chunks - 1, parts_x), (1, parts_z))
            ],
            [
                pltpu.VMEM((most, parts, block * parts_y, span), F32)
                for most, parts in ((chunks - 1, parts_z), (1, parts_x))
            ],
            [
                pltpu.VMEM((most, parts - 1, block * parts_y, span), F32)
                for most, parts in ((chunks - 1, parts_z), (1, parts_x))
            ],
            pltpu.VMEM((chunks, parts_y, block, span), F32),
            pltpu.VMEM((chunks, parts_y - 1, parts_y, block, span), F32),
            pltpu.VMEM((chunks, parts_y, block, span), F32),
            pltpu.VMEM((2, 1, span), F32),
            pltpu.VMEM((2, most, 1, span), F32),
            dma((9,)),
            pltpu.SemaphoreType.REGULAR((2,)),
            dma((2, LEVELS, 2)),
            dma((2, LEVELS, 2)),
            dma((chunks,)),
            dma((chunks,)),
            dma((chunks,)),
            dma((chunks,)),
            dma((chunks, parts_y - 1)),
            dma((chunks, parts_y - 1)),
            dma((2,)),
            dma((2,)),
        ],
        compiler_params=pltpu.CompilerParams(
            collective_id=0, has_side_effects=True, vmem_limit_bytes=56164352
        ),
    )(
        kappa,
        source_pair[0],
        adjoint_pair[0],
        wavelet[0],
        residuals[0],
        source_cell[0],
        jnp.transpose(receiver_cells, (1, 0, 2)),
    )
    return direction.reshape(depth, rows, span)


def solution(mesh):
    return jax.shard_map(
        functools.partial(per_device, mesh.shape["dom"]),
        mesh=mesh,
        in_specs=(
            P("dom", None, None),
            P("shot", None, "dom", None, None),
            P("shot", None, "dom", None, None),
            P("shot", None),
            P("shot", None, None),
            P("shot", None),
            P("shot", None, None),
        ),
        out_specs=P("dom", "shot", None),
        check_vma=False,
    )
```

```python
import functools

import jax
import jax.numpy as jnp
from jax import lax
from jax.experimental import pallas as pl
from jax.experimental.pallas import tpu as pltpu
from jax.sharding import PartitionSpec as P

MESH = pl.DeviceIdType.MESH
LEVELS = 4
HALO = 4
SCALE = 5040.0
RING = (8064.0, -1008.0, 128.0, -9.0)
CENTER = 3.0 * -14350.0
SHOT_PARTS = (2, 4, 8)
F32 = jnp.float32
BF16 = jnp.bfloat16


def split(value):
    high = value.astype(BF16)
    low = (value - high.astype(F32)).astype(BF16)
    return high, low


def band(size, weights):
    rows = lax.broadcasted_iota(jnp.int32, (size, size), 0)
    columns = lax.broadcasted_iota(jnp.int32, (size, size), 1)
    distance = jnp.abs(rows - columns)
    matrix = jnp.zeros((size, size), F32)
    for d, weight in enumerate(weights):
        matrix = jnp.where(distance == d, weight, matrix)
    return matrix


def twice(matrix, axis):
    matrix = matrix.astype(BF16)
    return jnp.concatenate((matrix, matrix), axis=axis)


def far_first(size):
    return sorted(range(1, size), key=lambda step: -min(step, size - step))


def dot(a, b):
    return jnp.dot(a, b, preferred_element_type=F32)


def rows_of(blocks):
    return jnp.concatenate(blocks, axis=0)


def columns_of(blocks):
    return jnp.concatenate(blocks, axis=1)


def kernel(
    doms, cells,
    kappa_hbm, source_hbm, adjoint_hbm, wave_hbm, residual_hbm, cell_hbm, receiver_hbm, out,
    wave, residual, cell, receiver, kappa, given, fields, totals, part, spot, marks, row_side, column_side, inject_side,
    blur_row, blur_column, order,
    first_in, second_out, second_in, y_out, y_in, y_sum, power_out, power_in,
    load_sem, known, halo_send, halo_recv,
    first_send, first_recv, second_send, second_recv, y_send, y_recv, p_send, p_recv,
):
    depth, width, span = kappa.shape
    shot, dom = lax.axis_index("shot"), lax.axis_index("dom")
    core = dom % 2
    anchor = dom * depth
    parts_y, parts_x, parts_z = SHOT_PARTS
    rows = width // (parts_y * parts_x * parts_z)
    z_at, x_at, y_at = shot % parts_z, shot // parts_z % parts_x, shot // (parts_z * parts_x)
    first_two = ((parts_x, parts_z), (parts_z, parts_x))
    ring = parts_y * doms // 2

    def by_x(step):
        return ((y_at * parts_x + (x_at + step) % parts_x) * parts_z + z_at, dom)

    def by_z(step):
        return ((y_at * parts_x + x_at) * parts_z + (z_at + step) % parts_z, dom)

    def by_y(step):
        return (((y_at + step) % parts_y * parts_x + x_at) * parts_z + z_at, dom)

    def by_x_and_dom(step):
        return (by_x(step // doms)[0], (dom + step) % doms)

    def by_ring(step, turn):
        at = (y_at * (doms // 2) + dom // 2 + step) % ring
        y_hi, chip = at // (doms // 2), at % (doms // 2)
        return ((y_hi * parts_x + x_at) * parts_z + z_at, chip * 2 + (core + turn) % 2)

    def near(size):
        return sorted({1, size - 1})

    def next_to(size):
        return [2, size - 2] if size > 4 else []

    loads = []
    for at, (source, target) in enumerate(
        (
            (source_hbm.at[0], given[0][0]),
            (adjoint_hbm.at[0], given[1][0]),
            (receiver_hbm, receiver),
            (residual_hbm, residual),
            (wave_hbm, wave),
            (cell_hbm, cell),
            (kappa_hbm, kappa),
            (source_hbm.at[1], given[0][1]),
            (adjoint_hbm.at[1], given[1][1]),
        )
    ):
        copy = pltpu.make_async_copy(source, target, load_sem.at[at])
        copy.start()
        loads.append(copy)

    barrier = pltpu.get_barrier_semaphore()
    stages = (
        [by_z(step) for step in far_first(parts_z)],
        [
            by_x_and_dom(step * doms + at)
            for step in far_first(parts_x) + [0]
            for at in range(doms)
            if step or at
        ],
    )
    beyond = [by_ring(step, 0) for step in near(ring)]
    beyond += [by_z(step) for step in near(parts_z)] + [by_x(step) for step in near(parts_x)]
    peers = [by_ring(2 * core - 1, 1), by_ring(0, 1)] + beyond
    farther = [by_ring(step, 0) for step in next_to(ring)]
    farther += [by_z(step) for step in next_to(parts_z)]
    for peer in peers:
        pl.semaphore_signal(barrier, inc=1, device_id=peer, device_id_type=MESH)

    def beside(side):
        neighbour = dom + 2 * side - 1
        return neighbour, (neighbour >= 0) & (neighbour < doms)

    def halo_copy(which, level, side, landing):
        field = fields[which][level]
        return pltpu.make_async_remote_copy(
            src_ref=field.at[pl.ds(HALO + (depth - HALO) * side, HALO)],
            dst_ref=field.at[pl.ds((HALO + depth) * landing, HALO)],
            send_sem=halo_send.at[which, level, side],
            recv_sem=halo_recv.at[which, level, landing],
            device_id=(shot, beside(side)[0]),
            device_id_type=MESH,
        )

    def halo_start(which, level, side):
        @pl.when(beside(side)[1])
        def _():
            halo_copy(which, level, side, 1 - side).start()

    def halo_wait(which, level, side):
        @pl.when(beside(side)[1])
        def _():
            halo_copy(which, level, side, side).wait_recv()

    for which in (0, 1):
        loads[which].wait()
        field = fields[which][LEVELS - 1]
        for start in (0, depth - HALO):
            field[start + HALO : start + 2 * HALO] = given[which][0][
                start : start + HALO
            ].astype(F32)
        if which == 0:
            pl.semaphore_wait(barrier, len(peers))
            for peer in beyond:
                pl.semaphore_signal(known.at[0], inc=1, device_id=peer, device_id_type=MESH)
        for turn in (0, 1):
            halo_start(which, LEVELS - 1, turn ^ core)
    @pl.when(dom == 0)
    def _():
        for which in (0, 1):
            for level in range(LEVELS):
                fields[which][level][0:HALO] = jnp.zeros((HALO, width, span), F32)

    @pl.when(dom == doms - 1)
    def _():
        for which in (0, 1):
            for level in range(LEVELS):
                fields[which][level][HALO + depth :] = jnp.zeros((HALO, width, span), F32)

    for which in (0, 1):
        fields[which][LEVELS - 1][2 * HALO : depth] = given[which][0][
            HALO : depth - HALO
        ].astype(F32)

    for load in loads[2:6]:
        load.wait()
    row_side[...] = twice(band(width, (0.0,) + RING), 1)
    column_side[...] = twice(band(span, (0.0,) + RING), 0)
    first = lax.broadcasted_iota(jnp.int32, (width, span), 0) == cell[1]
    second = lax.broadcasted_iota(jnp.int32, (width, span), 1) == cell[2]
    spot[...] = jnp.where(first & second, 1.0, 0.0)
    lines = lax.broadcasted_iota(jnp.int32, (span, receiver.shape[2]), 0)
    for level in range(1, LEVELS):
        spread = jnp.where(lines == receiver[2], residual[level : level + 1, :], 0.0)
        inject_side[level] = columns_of(split(jnp.transpose(spread)))
    lines = lax.broadcasted_iota(jnp.int32, (width, receiver.shape[2]), 0)

    @pl.loop(0, depth)
    def _(z):
        hit = (lines == receiver[1]) & (receiver[0] == anchor + z)
        marks[z] = jnp.where(hit, 1.0, 0.0).astype(BF16)

    place = lax.broadcasted_iota(jnp.int32, (width, width), 0)
    row = place % rows
    y_hi = place // rows % parts_y
    for way, parts in enumerate(first_two):
        minor = place // (rows * parts_y) % parts[1]
        major = place // (rows * parts_y * parts[1])
        x_of, z_of = (major, minor) if way == 0 else (minor, major)
        wanted = ((y_hi * parts_x + x_of) * parts_z + z_of) * rows + row
        distance = jnp.abs(wanted - lax.broadcasted_iota(jnp.int32, (width, width), 1))
        taps = jnp.zeros((width, width), F32)
        for d, weight in enumerate((0.375, 0.25, 0.0625)):
            taps = jnp.where(distance == d, weight, taps)
        blur_row[way] = twice(taps, 1)
    blur_column[...] = twice(band(span, (0.375, 0.25, 0.0625)), 0)
    for way, parts in enumerate(first_two):
        count = HALO * width // parts[0]
        place = lax.broadcasted_iota(jnp.int32, (count, count), 0)
        row = place % rows
        layer = place // rows % HALO
        y_hi = place // (rows * HALO) % parts_y
        minor = place // (rows * HALO * parts_y)
        wanted = ((layer * parts[1] + minor) * parts_y + y_hi) * rows + row
        hit = wanted == lax.broadcasted_iota(jnp.int32, (count, count), 1)
        order[way][...] = twice(jnp.where(hit, 1.0, 0.0), 1)

    def both_sides(blocks, left, right):
        flat = rows_of([columns_of(block) for block in blocks])
        upright = columns_of([rows_of(block) for block in blocks])
        flat, upright = dot(flat, right), dot(left, upright)
        return [
            flat[at * width : (at + 1) * width] + upright[:, at * span : (at + 1) * span]
            for at in range(len(blocks))
        ]

    def advance(which, level, start):
        field = fields[which][level]
        layers = range(HALO)
        if level == LEVELS - 1:
            blocks = [(given[which][0][start + at],) for at in layers]
            lateral = both_sides(blocks, row_side[:, :width], column_side[:span])
        else:
            blocks = [split(field[start + at + HALO]) for at in layers]
            lateral = both_sides(blocks, row_side[...], column_side[...])
        if which == 1:
            inject = dot(rows_of([marks[start + at] for at in layers]), inject_side[level])
            inject = inject[:, :span] + inject[:, span:]
            inject = [inject[at * width : (at + 1) * width] for at in layers]
        else:
            inject = [
                jnp.where(cell[0] == anchor + start + at, wave[level], 0.0) * spot[...]
                for at in layers
            ]
        blurred = []
        for at in layers:
            z = start + at
            current = field[z + HALO]
            summed = lateral[at] + CENTER * current
            for shift in range(1, HALO + 1):
                summed = summed + RING[shift - 1] * (
                    field[z + HALO + shift] + field[z + HALO - shift]
                )
            term = kappa[z] * (summed * (1.0 / SCALE)) + inject[at]
            if which == 0:
                product = fields[1][level][z + HALO] * term
                if level < LEVELS - 1:
                    product = product + totals[level][z]
                if level > 0:
                    totals[level - 1][z] = product
                else:
                    blurred.append(product)
            if level > 0:
                if level == LEVELS - 1:
                    later = given[which][1][z].astype(F32)
                else:
                    later = fields[which][level + 1][z + HALO]
                fields[which][level - 1][z + HALO] = 2.0 * current - later + term
        return blurred

    def blur(blurred, start, way):
        flat = dot(rows_of([columns_of(split(at)) for at in blurred]), blur_column[...])
        blocks = [flat[at * width : (at + 1) * width] for at in range(HALO)]
        upright = dot(blur_row[way], columns_of([rows_of(split(at)) for at in blocks]))
        for at in range(HALO):
            part[start + at] = upright[:, at * span : (at + 1) * span]

    def remote(source, target, send_sem, recv_sem, peer):
        return pltpu.make_async_remote_copy(
            src_ref=source,
            dst_ref=target,
            send_sem=send_sem,
            recv_sem=recv_sem,
            device_id=peer,
            device_id_type=MESH,
        )

    inner, outer = (depth - HALO) * (1 - core), (depth - HALO) * core
    starts = (HALO, 2 * HALO, inner, outer)
    ways = (1, 0, 0, 0)
    spots = (x_at, z_at)

    def first_copy(chunk, step):
        way = ways[chunk]
        stripe = width // first_two[way][0]
        place = (spots[way] + step) % first_two[way][0] * stripe
        return remote(
            part.at[pl.ds(starts[chunk], HALO), pl.ds(pl.multiple_of(place, stripe), stripe)],
            first_in[way].at[max(chunk - 1, 0), step - 1],
            first_send.at[chunk],
            first_recv.at[chunk],
            (by_x, by_z)[way](step),
        )

    def second_copy(chunk, step):
        way = ways[chunk]
        return remote(
            second_out[way].at[max(chunk - 1, 0), (spots[1 - way] + step) % first_two[way][1]],
            second_in[way].at[max(chunk - 1, 0), step - 1],
            second_send.at[chunk],
            second_recv.at[chunk],
            (by_z, by_x)[way](step),
        )

    def together(into, send_sem, recv_sem):
        return remote(into, into, send_sem, recv_sem, by_x(1))

    def first_all(chunk):
        into = first_in[ways[chunk]].at[max(chunk - 1, 0)]
        return together(into, first_send.at[chunk], first_recv.at[chunk])

    def second_all(chunk):
        into = second_in[ways[chunk]].at[max(chunk - 1, 0)]
        return together(into, second_send.at[chunk], second_recv.at[chunk])

    def y_copy(chunk, step):
        return remote(
            y_out.at[chunk],
            y_in.at[chunk, step - 1],
            y_send.at[chunk, step - 1],
            y_recv.at[chunk, step - 1],
            by_y(step),
        )

    def first_steps(chunk):
        return far_first(first_two[ways[chunk]][0])

    def second_steps(chunk):
        return far_first(first_two[ways[chunk]][1])

    def finish(chunk):
        start = starts[chunk]
        blur(advance(0, 0, start), start, ways[chunk])
        for step in first_steps(chunk):
            first_copy(chunk, step).start()

    def inside(which, level):
        @pl.loop(HALO, depth - HALO, step=HALO)
        def _(start):
            advance(which, level, start)

    def sides(which, level):
        @pl.loop(0, 2)
        def _(turn):
            side = turn ^ core
            halo_wait(which, level, side)
            advance(which, level, (depth - HALO) * side)
            if level > 1 or which == 0:
                halo_start(which, level - 1, side)

    for load in loads[6:]:
        load.wait()
    for level in reversed(range(2, LEVELS)):
        for which in (0, 1):
            inside(which, level)
            sides(which, level)
            if level == LEVELS - 1 and which == 0:
                pl.semaphore_wait(known.at[0], len(beyond))
                for peer in farther:
                    pl.semaphore_signal(known.at[1], inc=1, device_id=peer, device_id_type=MESH)
    inside(0, 1)
    advance(1, 1, starts[1])
    sides(0, 1)
    if farther:
        pl.semaphore_wait(known.at[1], len(farther))
    finish(1)
    advance(1, 1, starts[0])
    finish(0)
    for chunk, side in ((2, 1 - core), (3, core)):
        halo_wait(1, 1, side)
        advance(1, 1, starts[chunk])
        halo_wait(0, 0, side)
        finish(chunk)

    for level in reversed(range(LEVELS)):
        for which in (0, 1) if level > 0 else (0,):
            for side in (0, 1):

                @pl.when(beside(side)[1])
                def _():
                    halo_copy(which, level, side, 1 - side).wait_send()

    for chunk in (1, 2, 3, 0):
        way = ways[chunk]
        parts = first_two[way]
        stripe = width // parts[0]
        own = pl.multiple_of(spots[way] * stripe, stripe)
        summed = part[pl.ds(starts[chunk], HALO), pl.ds(own, stripe)]
        first_all(chunk).wait_recv()
        for step in first_steps(chunk):
            summed = summed + first_in[way][max(chunk - 1, 0), step - 1]
        moved = dot(order[way][...], rows_of(split(summed.reshape(HALO * stripe, span))))
        second_out[way][max(chunk - 1, 0)] = moved.reshape(parts[1], HALO * stripe // parts[1], span)
        for step in second_steps(chunk):
            second_copy(chunk, step).start()
    for chunk in range(len(starts)):
        first_all(chunk).wait_send()
    block = rows * HALO
    for chunk in (1, 2, 0, 3):
        way = ways[chunk]
        summed = second_out[way][max(chunk - 1, 0), spots[1 - way]]
        second_all(chunk).wait_recv()
        for step in second_steps(chunk):
            summed = summed + second_in[way][max(chunk - 1, 0), step - 1]
        y_out[chunk] = summed.reshape(parts_y, block, span)
        for step in range(1, parts_y):
            y_copy(chunk, step).start()
    power = jnp.zeros((block, span), F32)
    for chunk in (1, 2, 0, 3):
        summed = y_out[chunk]
        for step in range(1, parts_y):
            y_copy(chunk, step).wait_recv()
            summed = summed + y_in[chunk, step - 1]
        y_sum[chunk] = summed
        for y_hi in range(parts_y):
            power = power + summed[y_hi] * summed[y_hi]
    power = jnp.sum(power, axis=0, keepdims=True)
    for stage, peers in enumerate(stages):
        power_out[stage] = power
        for step, peer in enumerate(peers):
            remote(
                power_out.at[stage],
                power_in.at[stage, step],
                p_send.at[stage],
                p_recv.at[stage],
                peer,
            ).start()
        if stage == 0:
            for chunk in range(len(starts)):
                second_all(chunk).wait_send()
                for step in range(1, parts_y):
                    y_copy(chunk, step).wait_send()
        else:
            into = power_in.at[0, pl.ds(0, len(stages[0]))]
            together(into, p_send.at[0], p_recv.at[0]).wait_send()
        into = power_in.at[stage, pl.ds(0, len(peers))]
        together(into, p_send.at[stage], p_recv.at[stage]).wait_recv()
        for step in range(len(peers)):
            power = power + power_in[stage, step]
    scale = lax.rsqrt(jnp.full((1, 1), jnp.sum(power)) * (1.0 / cells) + 1e-6)
    for chunk, start in enumerate(starts):
        place = start * rows
        if not isinstance(place, int):
            place = pl.multiple_of(place, block)
        out[pl.ds(place, block)] = -y_sum[chunk, y_at] * scale

    into = power_in.at[1, pl.ds(0, len(stages[1]))]
    together(into, p_send.at[1], p_recv.at[1]).wait_send()


def per_device(doms, kappa, source_pair, adjoint_pair, wavelet, residuals, source_cell, receiver_cells):
    depth, width, span = kappa.shape
    receivers = receiver_cells.shape[2]
    parts_y, parts_x, parts_z = SHOT_PARTS
    rows = width // (parts_y * parts_x * parts_z)
    chunks = depth // HALO
    counts = (HALO * width // parts_x, HALO * width // parts_z)
    block = rows * HALO
    most = max(doms * parts_x, parts_z) - 1
    hbm = pl.BlockSpec(memory_space=pltpu.HBM)
    vmem = pl.BlockSpec(memory_space=pltpu.VMEM)
    dma = pltpu.SemaphoreType.DMA
    slab = pltpu.VMEM(kappa.shape, F32)
    padded = pltpu.VMEM((depth + 2 * HALO, width, span), F32)
    first = pltpu.VMEM(kappa.shape, BF16)
    direction = pl.pallas_call(
        functools.partial(kernel, doms, float(depth * doms * width * span)),
        out_shape=jax.ShapeDtypeStruct((depth * rows, span), F32),
        in_specs=[hbm] * 7,
        out_specs=vmem,
        scratch_shapes=[
            pltpu.SMEM(wavelet.shape[1:], F32),
            pltpu.VMEM(residuals.shape[1:], F32),
            pltpu.SMEM(source_cell.shape[1:], jnp.int32),
            pltpu.VMEM((3, 1, receivers), jnp.int32),
            slab,
            [[first] * 2] * 2,
            [[padded] * LEVELS] * 2,
            [slab] * (LEVELS - 1),
            slab,
            pltpu.VMEM((width, span), F32),
            pltpu.VMEM((depth, width, receivers), BF16),
            pltpu.VMEM((width, 2 * width), BF16),
            pltpu.VMEM((2 * span, span), BF16),
            pltpu.VMEM((LEVELS, receivers, 2 * span), BF16),
            pltpu.VMEM((2, width, 2 * width), BF16),
            pltpu.VMEM((2 * span, span), BF16),
            [pltpu.VMEM((count, 2 * count), BF16) for count in counts],
            [
                pltpu.VMEM((most, parts - 1, HALO, width // parts, span), F32)
                for most, parts in ((chunks - 1, parts_x), (1, parts_z))
            ],
            [
                pltpu.VMEM((most, parts, block * parts_y, span), F32)
                for most, parts in ((chunks - 1, parts_z), (1, parts_x))
            ],
            [
                pltpu.VMEM((most, parts - 1, block * parts_y, span), F32)
                for most, parts in ((chunks - 1, parts_z), (1, parts_x))
            ],
            pltpu.VMEM((chunks, parts_y, block, span), F32),
            pltpu.VMEM((chunks, parts_y - 1, parts_y, block, span), F32),
            pltpu.VMEM((chunks, parts_y, block, span), F32),
            pltpu.VMEM((2, 1, span), F32),
            pltpu.VMEM((2, most, 1, span), F32),
            dma((9,)),
            pltpu.SemaphoreType.REGULAR((2,)),
            dma((2, LEVELS, 2)),
            dma((2, LEVELS, 2)),
            dma((chunks,)),
            dma((chunks,)),
            dma((chunks,)),
            dma((chunks,)),
            dma((chunks, parts_y - 1)),
            dma((chunks, parts_y - 1)),
            dma((2,)),
            dma((2,)),
        ],
        compiler_params=pltpu.CompilerParams(
            collective_id=0, has_side_effects=True, vmem_limit_bytes=56164352
        ),
    )(
        kappa,
        source_pair[0],
        adjoint_pair[0],
        wavelet[0],
        residuals[0],
        source_cell[0],
        jnp.transpose(receiver_cells, (1, 0, 2)),
    )
    return direction.reshape(depth, rows, span)


def solution(mesh):
    return jax.shard_map(
        functools.partial(per_device, mesh.shape["dom"]),
        mesh=mesh,
        in_specs=(
            P("dom", None, None),
            P("shot", None, "dom", None, None),
            P("shot", None, "dom", None, None),
            P("shot", None),
            P("shot", None, None),
            P("shot", None),
            P("shot", None, None),
        ),
        out_specs=P("dom", "shot", None),
        check_vma=False,
    )
```
